128 devices in a mesh: win: 32 (over y, x_hi, z), seq: 4 (over x_lo, core).
Axes of the slice: x: 4 (x_hi: 2, x_lo: 2; x = x_hi * 2 + x_lo), y: 4, z: 4, core: 2. Of those that a mesh axis runs over, the one named last changes fastest.
Arguments:
- latent: float32 [32, 240, 5, 64], P('win', 'seq'), may hold values from -6 to 6
- frame_steps: int32 [32, 5], P('win'), may hold values from 0 to 49, as said below
- mod_table: float32 [50, 6, 1536], replicated, may hold values from -3 to 3
- w_patch: bfloat16 [64, 1536], replicated, may hold values from -0.75 to 0.75
- w_qkv: bfloat16 [1536, 4608], P(None, 'seq'), as said below
- w_out: bfloat16 [1536, 1536], P('seq'), may hold values from -0.15625 to 0.15625
- w_ff1: bfloat16 [1536, 8960], P(None, 'seq'), may hold values from -0.15625 to 0.15625
- w_ff2: bfloat16 [8960, 1536], P('seq'), may hold values from -0.0625 to 0.0625
- w_head: bfloat16 [1536, 64], replicated, may hold values from -0.15625 to 0.15625
Outputs:
- velocity: float32 [32, 240, 5, 64], P('win', 'seq')
- latent_next: float32 [32, 240, 5, 64], P('win', 'seq')
The draws below stay inside these ranges and needn't reach their ends.
Inputs may be any that keep to these rules, and one draw needn't show every extreme that they name: `frame_steps`: frames that neighbouring windows share carry the same index in both windows. `w_qkv`: columns come head by head, each as query, key, value of 128 columns.
All inputs are finite; a program needn't handle non-finite values.
Results may differ from the reference program's by a relative error of at most 0.012.
Values may be sent and summed in bfloat16 or wider, within the bound.
No kernel may reach another device: no remote copies, remote signals or barrier semaphores. Data moves between devices by JAX's collectives and lax.ppermute only.
A program may use at most 128 MiB of HBM per device.

```python
import jax
import jax.numpy as jnp
from jax import lax

D = 1536
HEADS = 12
HEAD_DIM = 128
FF = 8960
LAT_CH = 64
FRAMES = 5
INTERSECTION = 2
STEPS = 50
STRIDE = 3
WINDOWS = 32
PATCHES = 240
TOK_WIN = 1200
N_SEQ = 4


def draw_frame_steps(key, part):
    key = jax.random.fold_in(key, 11)
    total = WINDOWS * STRIDE + INTERSECTION
    timeline = jax.random.randint(key, (total,), 0, STEPS)
    timeline = timeline.at[0].set(STEPS - 1).at[total - 1].set(0)
    positions = jnp.arange(WINDOWS)[:, None] * STRIDE + jnp.arange(FRAMES)[None, :]
    return timeline[positions].astype(jnp.int32)


def draw_w_qkv(key, part):
    key = jax.random.fold_in(key, 7)
    base = jax.random.normal(key, (D, HEADS, 3, HEAD_DIM), jnp.float32) * D ** (-0.5)
    return base.reshape(D, 3 * D).astype(jnp.bfloat16)


def level_of(stream_key, dims, split, low, high):
    def one(axis_at, shards_of):
        draws = jax.random.uniform(jax.random.fold_in(jax.random.fold_in(stream_key, 6), axis_at), (shards_of,), jnp.float32, low / len(split), high / len(split))
        return jnp.repeat(jnp.exp(draws), dims[axis_at] // shards_of).reshape((-1,) + (1,) * (len(dims) - axis_at - 1))

    gain = one(*split[0])
    for cut in split[1:]:
        gain = gain * one(*cut)
    return gain


def scatter_about(key, shape, deviation, bound, cuts=(), held_as=jnp.bfloat16):
    entries = deviation * jax.random.normal(key, shape, jnp.float32)
    if cuts:
        entries = entries * level_of(key, shape, cuts, -0.22, 0.18)
    return jnp.clip(entries, -bound, bound).astype(held_as)


def setup_inputs(seed: int = 0) -> dict:
    key_list = jax.random.split(jax.random.key(seed), 10)
    return {
        "latent": scatter_about(key_list[0], (WINDOWS, PATCHES, FRAMES, LAT_CH), 1.0, 6.0, ((0, 32), (1, 4)), jnp.float32),
        "frame_steps": draw_frame_steps(jax.random.fold_in(key_list[9], 71), 0),
        "mod_table": scatter_about(key_list[2], (STEPS, 6, D), 0.5, 3.0, (), jnp.float32),
        "w_patch": scatter_about(key_list[3], (LAT_CH, D), LAT_CH ** -0.5, 0.75),
        "w_qkv": draw_w_qkv(jax.random.fold_in(key_list[9], 71), 0),
        "w_out": scatter_about(key_list[5], (D, D), D ** -0.5, 0.15625, ((0, 4),)),
        "w_ff1": scatter_about(key_list[6], (D, FF), D ** -0.5, 0.15625, ((1, 4),)),
        "w_ff2": scatter_about(key_list[7], (FF, D), FF ** -0.5, 0.0625, ((0, 4),)),
        "w_head": scatter_about(key_list[8], (D, LAT_CH), D ** -0.5, 0.15625),
    }


epsilon = 1e-06
shift_factor = 5.0

def layer_norm(values):
    centered = values - lax.optimization_barrier(jnp.mean(values, axis=-1, keepdims=True))
    variance = lax.optimization_barrier(jnp.mean(centered * centered, axis=-1, keepdims=True))
    return centered * lax.rsqrt(variance + epsilon)

def noise_level(step_index):
    fraction = 1.0 - step_index.astype(jnp.float32) / STEPS
    return shift_factor * fraction / (1.0 + (shift_factor - 1.0) * fraction)

def attend(projected, heads_here):
    count = projected.shape[0]
    grouped = projected.reshape(count, heads_here, 3, HEAD_DIM).transpose(1, 2, 0, 3)

    def single_head(block):
        scores = jnp.dot(block[0], block[1].T, preferred_element_type=jnp.float32) * HEAD_DIM ** (-0.5)
        weights = jax.nn.softmax(scores, axis=-1).astype(jnp.bfloat16)
        return jnp.dot(weights, block[2], preferred_element_type=jnp.float32).astype(jnp.bfloat16)
    mixed = lax.map(single_head, grouped)
    return mixed.transpose(1, 0, 2).reshape(count, heads_here * HEAD_DIM)

def reference(latent, frame_steps, mod_table, w_patch, w_qkv, w_out, w_ff1, w_ff2, w_head):
    modulation_all = mod_table[frame_steps]
    group_units = FF // N_SEQ

    def one_window(inputs):
        window_latent, modulation = inputs
        flat = window_latent.astype(jnp.bfloat16).reshape(TOK_WIN, LAT_CH)
        embed = jnp.dot(flat, w_patch, preferred_element_type=jnp.float32).reshape(PATCHES, FRAMES, D)
        normed1 = (layer_norm(embed) * (1.0 + modulation[None, :, 1]) + modulation[None, :, 0]).astype(jnp.bfloat16)
        projected = jnp.dot(normed1.reshape(TOK_WIN, D), w_qkv, preferred_element_type=jnp.float32).astype(jnp.bfloat16)
        attended = attend(projected, HEADS)
        attn_out = jnp.dot(attended, w_out, preferred_element_type=jnp.float32).reshape(PATCHES, FRAMES, D)
        hidden1 = embed + modulation[None, :, 2] * attn_out
        normed2 = (layer_norm(hidden1) * (1.0 + modulation[None, :, 4]) + modulation[None, :, 3]).astype(jnp.bfloat16)
        inner = jax.nn.gelu(jnp.dot(normed2.reshape(TOK_WIN, D), w_ff1, preferred_element_type=jnp.float32), approximate=True).astype(jnp.bfloat16)
        ffn = jnp.zeros((TOK_WIN, D), jnp.float32)
        for group in range(N_SEQ):
            partial_sum = jnp.dot(inner[:, group * group_units:(group + 1) * group_units], w_ff2[group * group_units:(group + 1) * group_units], preferred_element_type=jnp.float32)
            rounded = lax.optimization_barrier(partial_sum.astype(jnp.bfloat16))
            ffn = ffn + rounded.astype(jnp.float32)
        hidden2 = hidden1 + modulation[None, :, 5] * ffn.reshape(PATCHES, FRAMES, D)
        normed3 = layer_norm(hidden2).astype(jnp.bfloat16)
        raw = jnp.dot(normed3.reshape(TOK_WIN, D), w_head, preferred_element_type=jnp.float32)
        return raw.reshape(PATCHES, FRAMES, LAT_CH)
    raw_all = lax.map(one_window, (latent, modulation_all))
    empty_window = jnp.zeros((1, PATCHES, FRAMES, LAT_CH), jnp.float32)
    left_source = jnp.concatenate([empty_window, raw_all[:-1]], axis=0)
    right_source = jnp.concatenate([raw_all[1:], empty_window], axis=0)
    rest = jnp.zeros((WINDOWS, PATCHES, FRAMES - INTERSECTION, LAT_CH), jnp.float32)
    left_full = jnp.concatenate([left_source[:, :, STRIDE:], rest], axis=2)
    right_full = jnp.concatenate([rest, right_source[:, :, :INTERSECTION]], axis=2)
    frame_index = jnp.arange(FRAMES)[None, :]
    window_index = jnp.arange(WINDOWS)[:, None]
    left_weight = jnp.where((frame_index < INTERSECTION) & (window_index > 0), 1.0 - (frame_index + 1.0) / (INTERSECTION + 1.0), 0.0)
    right_weight = jnp.where((frame_index >= STRIDE) & (window_index < WINDOWS - 1), 1.0 - (FRAMES - frame_index) / (INTERSECTION + 1.0), 0.0)
    own_weight = 1.0 - left_weight - right_weight
    velocity = own_weight[:, None, :, None] * raw_all + left_weight[:, None, :, None] * left_full + right_weight[:, None, :, None] * right_full
    step_size = noise_level(frame_steps + 1) - noise_level(frame_steps)
    latent_next = latent + step_size[:, None, :, None] * velocity
    return (velocity, latent_next)
```

```python
import functools

import jax
import jax.numpy as jnp
from jax import lax
from jax.experimental import pallas as pl
from jax.experimental.pallas import tpu as pltpu
from jax.sharding import PartitionSpec as P

HEAD_DIM = 128
INTERSECTION = 2
STEPS = 50
PERIOD = 40

epsilon = 1e-06
shift_factor = 5.0
bf16 = jnp.bfloat16
f32 = jnp.float32
AXES = ("win", "seq")
NT = (((1,), (1,)), ((), ()))
VMEM_LIMIT = 56 * 2**20


def place_of(index):
    win, seq = divmod(index, 4)
    y, rest = divmod(win, 8)
    x_hi, z = divmod(rest, 4)
    x_lo, core = divmod(seq, 2)
    return x_hi * 2 + x_lo, y, z, core


def index_of(x, y, z, core):
    x_hi, x_lo = divmod(x % 4, 2)
    return ((y * 2 + x_hi) * 4 + z) * 4 + x_lo * 2 + core


def moves(count, target):
    return [(i, index_of(*target(*place_of(i)))) for i in range(count)]


def to_sibling(x, y, z, core):
    return x, y, z, 1 - core


def to_chip(x, y, z, core):
    return x ^ 1, y, z, core


def to_cross(x, y, z, core):
    return x ^ 1, y, z, 1 - core


def to_partner(x, y, z, core):
    near = x ^ 1
    far = x - 1 if x % 2 == 0 else x + 1
    return (near if core == 0 else far), y, z, core


def noise_level(step_index):
    fraction = 1.0 - step_index.astype(f32) / STEPS
    return shift_factor * fraction / (1.0 + (shift_factor - 1.0) * fraction)


def row_groups(rows):
    return [(start, min(2 * PERIOD, rows - start)) for start in range(0, rows, 2 * PERIOD)]


def tiled(pattern, rows):
    pieces = [pattern] * (rows // PERIOD)
    if rows % PERIOD:
        pieces.append(pattern[: rows % PERIOD])
    return jnp.concatenate(pieces, axis=0) if len(pieces) > 1 else pieces[0]


def normalized(values):
    centered = values - jnp.mean(values, axis=-1, keepdims=True)
    variance = jnp.mean(centered * centered, axis=-1, keepdims=True)
    return centered * lax.rsqrt(variance + epsilon)


def gelu(x):
    inside = x * (0.7978845608028654 + 0.035677408136300125 * (x * x))
    half = 0.5 * x
    return half + half * jnp.tanh(inside)


def in_vmem(count):
    return [pl.BlockSpec(memory_space=pltpu.VMEM)] * count


def params():
    return pltpu.CompilerParams(vmem_limit_bytes=VMEM_LIMIT)


def cost(flops, size):
    return pl.CostEstimate(flops=int(flops), bytes_accessed=int(size), transcendentals=0)


def modulation_kernel(steps_ref, table_ref, out_ref):
    frame = lax.broadcasted_iota(jnp.int32, (PERIOD, 1), 0) % 5
    for j in range(out_ref.shape[0]):
        tile = jnp.zeros(out_ref.shape[1:], f32)
        for f in range(5):
            row = table_ref[j, pl.ds(steps_ref[0, f], 1), :]
            tile = jnp.where(frame == f, row, tile)
        out_ref[j] = tile


def modulation_rows(steps, table):
    return pl.pallas_call(
        modulation_kernel,
        out_shape=jax.ShapeDtypeStruct((table.shape[0], PERIOD, table.shape[2]), f32),
        in_specs=[pl.BlockSpec(memory_space=pltpu.SMEM)] + in_vmem(1),
        out_specs=in_vmem(1)[0],
        compiler_params=params(),
        name="modulation",
    )(steps, table)


def project_kernel(blocks, scale, *refs):
    lat_refs = refs[:blocks]
    mod_ref, w_patch_ref, w_qkv_ref = refs[blocks : blocks + 3]
    out_refs = refs[blocks + 3 : 2 * blocks + 3]
    normed_ref = refs[2 * blocks + 3]
    rows = lat_refs[0].shape[0]
    for b in range(blocks):
        for start, count in row_groups(rows):
            embed = jnp.dot(
                lat_refs[b][start : start + count, :],
                w_patch_ref[...],
                preferred_element_type=f32,
            )
            value = normalized(embed) * (1.0 + tiled(mod_ref[1], count)) + tiled(mod_ref[0], count)
            normed_ref[b, start : start + count, :] = value.astype(bf16)
        for c in range(w_qkv_ref.shape[1] // HEAD_DIM):
            columns = slice(c * HEAD_DIM, (c + 1) * HEAD_DIM)
            part = jnp.dot(normed_ref[b], w_qkv_ref[:, columns], preferred_element_type=f32)
            if c % 3 == 0:
                part = part * scale
            out_refs[b][:, columns] = part.astype(bf16)


def project(lats, mods, w_patch, w_qkv, scale):
    blocks = len(lats)
    rows = lats[0].shape[0]
    width, columns = w_qkv.shape
    return pl.pallas_call(
        functools.partial(project_kernel, blocks, scale),
        out_shape=[jax.ShapeDtypeStruct((rows, columns), bf16)] * blocks,
        in_specs=in_vmem(blocks + 3),
        out_specs=in_vmem(blocks),
        scratch_shapes=[pltpu.VMEM((blocks, rows, width), bf16)],
        compiler_params=params(),
        cost_estimate=cost(2 * blocks * rows * width * columns, 2 * width * columns),
        name="project",
    )(*lats, mods, w_patch, w_qkv)


def attend_kernel(queries, heads, real, *refs):
    qkv_refs = refs[:4]
    out_refs = refs[4 : 4 + len(queries)]
    key_ref, value_ref = refs[4 + len(queries) :]
    rows = qkv_refs[0].shape[0]
    is_real = lax.broadcasted_iota(jnp.int32, (rows, 1), 0) < real
    for h in range(heads):
        for b in range(4):
            where = slice(b * rows, (b + 1) * rows)
            key_ref[h, where, :] = qkv_refs[b][:, (3 * h + 1) * HEAD_DIM : (3 * h + 2) * HEAD_DIM]
            value = qkv_refs[b][:, (3 * h + 2) * HEAD_DIM : (3 * h + 3) * HEAD_DIM]
            value_ref[h, where, :HEAD_DIM] = jnp.where(is_real, value, jnp.zeros_like(value))
            ones = jnp.where(is_real, jnp.ones_like(value), jnp.zeros_like(value))
            value_ref[h, where, HEAD_DIM:] = ones
    for i, b in enumerate(queries):
        for h in range(heads):
            query = qkv_refs[b][:, 3 * h * HEAD_DIM : (3 * h + 1) * HEAD_DIM]
            scores = lax.dot_general(query, key_ref[h], NT, preferred_element_type=f32)
            top = jnp.max(scores, axis=1, keepdims=True)
            weights = jnp.exp2(scores - top).astype(bf16)
            both = jnp.dot(weights, value_ref[h], preferred_element_type=f32)
            out = both[:, :HEAD_DIM] / both[:, HEAD_DIM:]
            out_refs[i][:, h * HEAD_DIM : (h + 1) * HEAD_DIM] = out.astype(bf16)


def attend(qkvs, queries, heads, real):
    rows = qkvs[0].shape[0]
    return pl.pallas_call(
        functools.partial(attend_kernel, queries, heads, real),
        out_shape=[jax.ShapeDtypeStruct((rows, heads * HEAD_DIM), bf16)] * len(queries),
        in_specs=in_vmem(4),
        out_specs=in_vmem(len(queries)),
        scratch_shapes=[
            pltpu.VMEM((heads, 4 * rows, HEAD_DIM), bf16),
            pltpu.VMEM((heads, 4 * rows, 2 * HEAD_DIM), bf16),
        ],
        compiler_params=params(),
        cost_estimate=cost(8 * heads * len(queries) * rows * 4 * rows * 2 * HEAD_DIM, 2**20),
        name="attend",
    )(*qkvs)


def output_kernel(a0, a1, a2, a3, w0, w1, w2, w3, lat_ref, mod_ref, w_patch_ref, hid_ref, norm_ref):
    pairs = ((a0, w0), (a1, w1), (a2, w2), (a3, w3))
    for start, count in row_groups(lat_ref.shape[0]):
        rows = slice(start, start + count)
        total = None
        for a_ref, w_ref in pairs:
            part = jnp.dot(a_ref[rows, :], w_ref[...], preferred_element_type=f32)
            total = part if total is None else total + part
        embed = jnp.dot(lat_ref[rows, :], w_patch_ref[...], preferred_element_type=f32)
        hidden = embed + tiled(mod_ref[2], count) * total
        hid_ref[rows, :] = hidden
        value = normalized(hidden) * (1.0 + tiled(mod_ref[4], count)) + tiled(mod_ref[3], count)
        norm_ref[rows, :] = value.astype(bf16)


def output(attended, weights, lat, mods, w_patch):
    shape = (lat.shape[0], w_patch.shape[1])
    return pl.pallas_call(
        output_kernel,
        out_shape=[jax.ShapeDtypeStruct(shape, f32), jax.ShapeDtypeStruct(shape, bf16)],
        in_specs=in_vmem(11),
        out_specs=in_vmem(2),
        compiler_params=params(),
        cost_estimate=cost(2 * shape[0] * shape[1] ** 2, 2 * shape[1] ** 2),
        name="output",
    )(*attended, *weights, lat, mods, w_patch)


def unit_chunks(units):
    return [(start, min(512, units - start)) for start in range(0, units, 512)]


def ffn_kernel(residual, *refs):
    if residual:
        x_ref, hid_ref, mod_ref = refs[:3]
        refs = refs[3:]
    else:
        x_ref = refs[0]
        refs = refs[1:]
    up = refs[0:2]
    down = refs[2:4]
    out_ref, up_buf, down_buf, acc_ref, up_sem, down_sem = refs[4:]
    units = up[0].shape[0]
    parts = unit_chunks(units)
    copies = []
    for half in range(2):
        for start, count in parts:
            i = len(copies)
            source = pl.ds(start, count)
            target = pl.ds(half * units + start, count)
            copies.append(
                (
                    pltpu.make_async_copy(up[half].at[source], up_buf.at[target], up_sem.at[i]),
                    pltpu.make_async_copy(down[half].at[source], down_buf.at[target], down_sem.at[i]),
                )
            )
    for first, second in copies:
        first.start()
        second.start()
    i = 0
    for half in range(2):
        for start, count in parts:
            where = slice(half * units + start, half * units + start + count)
            copies[i][0].wait()
            inner = lax.dot_general(x_ref[...], up_buf[where, :], NT, preferred_element_type=f32)
            inner = gelu(inner).astype(bf16)
            copies[i][1].wait()
            part = jnp.dot(inner, down_buf[where, :], preferred_element_type=f32)
            acc_ref[...] = part if i == 0 else acc_ref[...] + part
            i += 1
    if residual:
        for start, count in row_groups(x_ref.shape[0]):
            rows = slice(start, start + count)
            value = hid_ref[rows, :] + tiled(mod_ref[5], count) * acc_ref[rows, :]
            out_ref[rows, :] = value.astype(out_ref.dtype)
    else:
        out_ref[...] = acc_ref[...]


def feed_forward(x, ups, downs, extra=()):
    rows, width = x.shape
    units = ups[0].shape[0]
    count = 2 * len(unit_chunks(units))
    return pl.pallas_call(
        functools.partial(ffn_kernel, bool(extra)),
        out_shape=jax.ShapeDtypeStruct(x.shape, bf16 if extra else f32),
        in_specs=in_vmem(1 + len(extra)) + [pl.BlockSpec(memory_space=pl.ANY)] * 4,
        out_specs=in_vmem(1)[0],
        scratch_shapes=[
            pltpu.VMEM((2 * units, width), bf16),
            pltpu.VMEM((2 * units, width), bf16),
            pltpu.VMEM((rows, width), f32),
            pltpu.SemaphoreType.DMA((count,)),
            pltpu.SemaphoreType.DMA((count,)),
        ],
        compiler_params=params(),
        cost_estimate=cost(8 * rows * width * units, 8 * units * width),
        name="feed_forward",
    )(x, *extra, *ups, *downs)


def head_kernel(ffn_ref, hid_ref, gate_ref, w_ref, out_ref):
    for start, count in row_groups(ffn_ref.shape[0]):
        rows = slice(start, start + count)
        hidden = hid_ref[rows, :].astype(f32) + tiled(gate_ref[0], count) * ffn_ref[rows, :]
        value = normalized(hidden).astype(bf16)
        out_ref[rows, :] = lax.dot_general(value, w_ref[...], NT, preferred_element_type=f32)


def head(ffn, hidden, gate, w_head_t):
    return pl.pallas_call(
        head_kernel,
        out_shape=jax.ShapeDtypeStruct((ffn.shape[0], w_head_t.shape[0]), f32),
        in_specs=in_vmem(4),
        out_specs=in_vmem(1)[0],
        compiler_params=params(),
        name="head",
    )(ffn, hidden, gate, w_head_t)


def body(latent, frame_steps, mod_table, w_patch, w_qkv, w_out, w_ff1, w_ff2, w_head):
    _, patches, frames, channels = latent.shape
    windows = lax.axis_size("win")
    devices = windows * lax.axis_size("seq")
    real = patches * frames
    rows = -(-real // 16) * 16
    heads = w_out.shape[0] // HEAD_DIM

    def send(value, target):
        return lax.ppermute(value, AXES, moves(devices, target))

    flat = latent.reshape(real, channels)
    lat = flat.astype(bf16)
    lat = jnp.concatenate([lat, lat[real - frames : real - frames + rows - real]], axis=0)
    lat_sib = send(lat, to_sibling)
    lat_chip = send(lat, to_chip)
    lat_cross = send(lat, to_cross)
    steps_partner = send(frame_steps, to_partner)

    table = jnp.transpose(mod_table, (1, 0, 2))
    mods = modulation_rows(frame_steps, table)
    gate_partner = modulation_rows(steps_partner, table[5:6])

    scale = HEAD_DIM**-0.5 * 1.4426950408889634
    (own,) = project([lat], mods, w_patch, w_qkv, scale)
    others = project([lat_sib, lat_chip, lat_cross], mods, w_patch, w_qkv, scale)
    qkvs = [own] + list(others)

    up = w_ff1.T
    up_sib = send(up, to_sibling)
    down_sib = send(w_ff2, to_sibling)
    out_sib = send(w_out, to_sibling)
    out_chip = send(w_out, to_partner)
    out_cross = send(out_chip, to_sibling)

    att_cross, att_chip = attend(qkvs, (3, 2), heads, real)
    got_cross = send(att_cross, to_cross)
    got_chip = send(att_chip, to_chip)
    att_sib, att_own = attend(qkvs, (1, 0), heads, real)
    got_sib = send(att_sib, to_sibling)

    hidden1, normed2 = output(
        (att_own, got_sib, got_chip, got_cross),
        (w_out, out_sib, out_chip, out_cross),
        lat,
        mods,
        w_patch,
    )
    normed_partner = send(normed2, to_partner)
    ups, downs = (up, up_sib), (w_ff2, down_sib)
    hidden_near = feed_forward(normed2, ups, downs, (hidden1, mods))
    hidden_partner = send(hidden_near, to_partner)
    ffn_partner = feed_forward(normed_partner, ups, downs)
    raw_partner = head(ffn_partner, hidden_partner, gate_partner, w_head.T)

    owner = [to for _, to in moves(devices, to_partner)]
    up_next = [(i, owner[i] + 4) for i in range(devices) if owner[i] + 4 < devices]
    down_next = [(i, owner[i] - 4) for i in range(devices) if owner[i] - 4 >= 0]
    raw16 = raw_partner.astype(bf16)
    raw = send(raw_partner, to_partner)[:real]
    before = lax.ppermute(raw16, AXES, up_next)[:real].astype(f32)
    after = lax.ppermute(raw16, AXES, down_next)[:real].astype(f32)

    window = lax.axis_index("win")
    frame = jnp.arange(frames)
    left = jnp.where(
        (frame < INTERSECTION) & (window > 0), 1.0 - (frame + 1.0) / (INTERSECTION + 1.0), 0.0
    )
    right = jnp.where(
        (frame >= frames - INTERSECTION) & (window < windows - 1),
        1.0 - (frames - frame) / (INTERSECTION + 1.0),
        0.0,
    )
    step_size = (noise_level(frame_steps + 1) - noise_level(frame_steps))[0]

    def per_row(v):
        return jnp.tile(v.astype(f32), patches)[:, None]

    stride = frames - INTERSECTION
    none = jnp.zeros((stride, channels), f32)
    from_left = jnp.concatenate([before[stride:], none], axis=0)
    from_right = jnp.concatenate([none, after[:-stride]], axis=0)
    velocity = (
        per_row(1.0 - left - right) * raw + per_row(left) * from_left + per_row(right) * from_right
    )
    latent_next = flat + per_row(step_size) * velocity
    shape = latent.shape
    return velocity.reshape(shape), latent_next.reshape(shape)


def solution(mesh):
    in_specs = (
        P("win", "seq", None, None),
        P("win", None),
        P(),
        P(),
        P(None, "seq"),
        P("seq", None),
        P(None, "seq"),
        P("seq", None),
        P(),
    )
    out_specs = (P("win", "seq", None, None), P("win", "seq", None, None))
    return jax.shard_map(body, mesh=mesh, in_specs=in_specs, out_specs=out_specs, check_vma=False)
```

```python
import functools

import jax
import jax.numpy as jnp
from jax import lax
from jax.experimental import pallas as pl
from jax.experimental.pallas import tpu as pltpu
from jax.sharding import PartitionSpec as P

HEAD_DIM = 128
INTERSECTION = 2
STEPS = 50
PERIOD = 40

epsilon = 1e-06
shift_factor = 5.0
bf16 = jnp.bfloat16
f32 = jnp.float32
AXES = ("win", "seq")
NT = (((1,), (1,)), ((), ()))
MIB = 2**20


def place_of(index):
    win, seq = divmod(index, 4)
    y, rest = divmod(win, 8)
    x_hi, z = divmod(rest, 4)
    x_lo, core = divmod(seq, 2)
    return x_hi * 2 + x_lo, y, z, core


def index_of(x, y, z, core):
    x_hi, x_lo = divmod(x % 4, 2)
    return ((y * 2 + x_hi) * 4 + z) * 4 + x_lo * 2 + core


def moves(count, target):
    return [(i, index_of(*target(*place_of(i)))) for i in range(count)]


def to_sibling(x, y, z, core):
    return x, y, z, 1 - core


def to_chip(x, y, z, core):
    return x ^ 1, y, z, core


def to_cross(x, y, z, core):
    return x ^ 1, y, z, 1 - core


def to_partner(x, y, z, core):
    near = x ^ 1
    far = x - 1 if x % 2 == 0 else x + 1
    return (near if core == 0 else far), y, z, core


barrier = lax.optimization_barrier


def row_groups(rows):
    return [(start, min(2 * PERIOD, rows - start)) for start in range(0, rows, 2 * PERIOD)]


def tiled(pattern, rows):
    pieces = [pattern] * (rows // PERIOD)
    if rows % PERIOD:
        pieces.append(pattern[: rows % PERIOD])
    return jnp.concatenate(pieces, axis=0) if len(pieces) > 1 else pieces[0]


def normalized(values):
    centered = values - jnp.mean(values, axis=-1, keepdims=True)
    variance = jnp.mean(centered * centered, axis=-1, keepdims=True)
    return centered * lax.rsqrt(variance + epsilon)


def gelu(x):
    inside = x * (0.7978845608028654 + 0.035677408136300125 * (x * x))
    half = 0.5 * x
    return half + half * jnp.tanh(inside)


def in_vmem(count):
    return [pl.BlockSpec(memory_space=pltpu.VMEM)] * count


def params(size):
    return pltpu.CompilerParams(vmem_limit_bytes=size * MIB)


def anywhere(count):
    return [pl.BlockSpec(memory_space=pl.ANY)] * count


def cost(flops, size):
    return pl.CostEstimate(flops=int(flops), bytes_accessed=int(size), transcendentals=0)


def rows_of_frames(steps_ref, table_ref, j):
    frame = lax.broadcasted_iota(jnp.int32, (8, 1), 0)
    vectors = [table_ref[j, pl.ds(steps_ref[0, f], 1), :] for f in range(5)]
    pieces = []
    for part in range(5):
        at = (frame + 8 * part) % 5
        tile = jnp.broadcast_to(vectors[0], (8, vectors[0].shape[1]))
        for f in range(1, 5):
            tile = jnp.where(at == f, vectors[f], tile)
        pieces.append(tile)
    return jnp.concatenate(pieces, axis=0)


def modulation_kernel(steps_ref, table_ref, first_ref, second_ref, last_ref):
    for j in range(6):
        out_ref, at = ((first_ref, j), (second_ref, j - 2), (last_ref, 0))[(j > 1) + (j > 4)]
        out_ref[at] = rows_of_frames(steps_ref, table_ref, j)


def modulation_rows(steps, table):
    return pl.pallas_call(
        modulation_kernel,
        out_shape=[jax.ShapeDtypeStruct((n, PERIOD, table.shape[2]), f32) for n in (2, 3, 1)],
        in_specs=[pl.BlockSpec(memory_space=pltpu.SMEM)] + in_vmem(1),
        out_specs=in_vmem(3),
        compiler_params=params(8),
        name="modulation",
    )(steps, table)


def project_block(lat_ref, mod_ref, w_patch_ref, w_qkv_ref, normed_ref, store):
    half, lanes = lat_ref.shape
    channels = lanes // 2
    for side in range(2):
        lat = lat_ref[:, side * channels : (side + 1) * channels]
        embed = jnp.dot(lat, w_patch_ref[...], preferred_element_type=f32)
        normed_ref[side * half : (side + 1) * half, :] = embed
    normed = []
    for start, count in row_groups(2 * half):
        value = normalized(normed_ref[start : start + count, :])
        value = value * (1.0 + tiled(mod_ref[1], count)) + tiled(mod_ref[0], count)
        normed.append(value.astype(bf16))
    normed = jnp.concatenate(normed, axis=0)
    columns = w_qkv_ref.shape[1]
    for c in range(0, columns, 256):
        end = min(c + 256, columns)
        part = jnp.dot(normed, w_qkv_ref[:, c:end], preferred_element_type=f32)
        for d in range(c, end, HEAD_DIM):
            h, j = divmod(d // HEAD_DIM, 3)
            store(h, j, part[:, d - c : d - c + HEAD_DIM])


def store_block(b, real, scale, query_ref, key_ref, value_ref):
    rows = query_ref.shape[0]
    where = slice(b * rows, (b + 1) * rows)

    def store(h, j, piece):
        if j == 0:
            query_ref[:, h * HEAD_DIM : (h + 1) * HEAD_DIM] = (piece * scale).astype(bf16)
        elif j == 1:
            key_ref[h, where, :] = piece.astype(bf16)
        else:
            at = lax.broadcasted_iota(jnp.int32, piece.shape, 0) < real
            value_ref[h, where, :HEAD_DIM] = jnp.where(at, piece, 0.0).astype(bf16)
            value_ref[h, where, HEAD_DIM:] = jnp.where(at, 1.0, 0.0).astype(bf16)

    return store


def project_kernel(blocks, placed, real, scale, after, *refs):
    lat_refs = refs[:blocks]
    mod_ref, w_patch_ref, w_qkv_ref = refs[blocks : blocks + 3]
    refs = refs[blocks + 3 :]
    if placed:
        key_in, value_in = refs[:2]
        refs = refs[2:]
    refs = refs[after:]
    query_refs = refs[:blocks]
    key_ref, value_ref, embed_ref = refs[blocks:]
    rows = query_refs[0].shape[0]
    if placed:
        key_ref[:, : placed * rows, :] = key_in[...]
        value_ref[:, : placed * rows, :] = value_in[...]
    for b in range(blocks):
        store = store_block(placed + b, real, scale, query_refs[b], key_ref, value_ref)
        project_block(lat_refs[b], mod_ref, w_patch_ref, w_qkv_ref, embed_ref, store)


def project(lats, mods, w_patch, w_qkv, real, scale, before=(), after=()):
    blocks = len(lats)
    rows = 2 * lats[0].shape[0]
    width, columns = w_qkv.shape
    heads = columns // (3 * HEAD_DIM)
    placed = before[0].shape[1] // rows if before else 0
    tokens = (placed + blocks) * rows
    return pl.pallas_call(
        functools.partial(project_kernel, blocks, placed, real, scale, len(after)),
        out_shape=[jax.ShapeDtypeStruct((rows, heads * HEAD_DIM), bf16)] * blocks
        + [
            jax.ShapeDtypeStruct((heads, tokens, HEAD_DIM), bf16),
            jax.ShapeDtypeStruct((heads, tokens, 2 * HEAD_DIM), bf16),
        ],
        in_specs=in_vmem(blocks + 3 + len(before)) + anywhere(len(after)),
        out_specs=in_vmem(blocks + 2),
        scratch_shapes=[pltpu.VMEM((rows, width), f32)],
        compiler_params=params(8),
        cost_estimate=cost(rows, rows),
        name="project",
    )(*lats, mods, w_patch, w_qkv, *before, *after)


def attend_kernel(blocks, after, *refs):
    query_refs = refs[:blocks]
    key_ref, value_ref = refs[blocks : blocks + 2]
    out_refs = refs[blocks + 2 + after :]
    for query_ref, out_ref in zip(query_refs, out_refs):
        for h in range(key_ref.shape[0]):
            columns = slice(h * HEAD_DIM, (h + 1) * HEAD_DIM)
            query = query_ref[:, columns]
            scores = lax.dot_general(query, key_ref[h], NT, preferred_element_type=f32)
            top = jnp.max(scores, axis=1, keepdims=True)
            weights = jnp.exp2(scores - top).astype(bf16)
            both = jnp.dot(weights, value_ref[h], preferred_element_type=f32)
            out_ref[:, columns] = (both[:, :HEAD_DIM] / both[:, HEAD_DIM:]).astype(bf16)


def attend(queries, keys, values, after=()):
    blocks = len(queries)
    rows, width = queries[0].shape
    return pl.pallas_call(
        functools.partial(attend_kernel, blocks, len(after)),
        out_shape=[jax.ShapeDtypeStruct((rows, width), bf16)] * blocks,
        in_specs=in_vmem(blocks + 2) + anywhere(len(after)),
        out_specs=in_vmem(blocks),
        compiler_params=params(8),
        cost_estimate=cost(16 * blocks * rows * width * 4 * rows, 2**20),
        name="attend",
    )(*queries, keys, values, *after)


def output_kernel(a0, a1, a2, a3, w0, w1, w2, w3, lat_ref, mod_ref, w_patch_ref, hid_ref, norm_ref):
    attended = jnp.concatenate([a[...] for a in (a0, a1, a2, a3)], axis=1)
    width = hid_ref.shape[1]
    for c in range(0, width, 256):
        where = slice(c, c + 256)
        weight = jnp.concatenate([w[:, where] for w in (w0, w1, w2, w3)], axis=0)
        total = jnp.dot(attended, weight, preferred_element_type=f32)
        channels = lat_ref.shape[1] // 2
        lat = jnp.concatenate([lat_ref[:, :channels], lat_ref[:, channels:]], axis=0)
        embed = jnp.dot(lat, w_patch_ref[:, where], preferred_element_type=f32)
        gate = tiled(mod_ref[0, :, where], hid_ref.shape[0])
        hid_ref[:, where] = embed + gate * total
    for start, count in row_groups(hid_ref.shape[0]):
        rows = slice(start, start + count)
        value = normalized(hid_ref[rows, :]) * (1.0 + tiled(mod_ref[2], count))
        norm_ref[rows, :] = (value + tiled(mod_ref[1], count)).astype(bf16)


def output(attended, weights, lat, mods, w_patch):
    shape = (2 * lat.shape[0], w_patch.shape[1])
    return pl.pallas_call(
        output_kernel,
        out_shape=[jax.ShapeDtypeStruct(shape, f32), jax.ShapeDtypeStruct(shape, bf16)],
        in_specs=in_vmem(11),
        out_specs=in_vmem(2),
        compiler_params=params(8),
        cost_estimate=cost(2 * shape[0] * shape[1] ** 2, 2 * shape[1] ** 2),
        name="output",
    )(*attended, *weights, lat, mods, w_patch)


UNITS = 512
COLUMNS = 256


def ffn_kernel(residual, *refs):
    if residual:
        x_ref, hid_ref, mod_ref = refs[:3]
        refs = refs[3:]
    else:
        x_ref = refs[0]
        refs = refs[1:]
    up = refs[0:2]
    down = refs[2:4]
    out_ref, inner_ref = refs[4:]
    units = up[0].shape[0]
    width = x_ref.shape[1]
    for half in range(2):
        for start in range(0, units, UNITS):
            end = min(start + UNITS, units)
            weight = up[half][start:end, :]
            inner = lax.dot_general(x_ref[...], weight, NT, preferred_element_type=f32)
            inner_ref[half, :, start:end] = gelu(inner).astype(bf16)
    for start in range(0, width, COLUMNS):
        where = slice(start, start + COLUMNS)
        value = jnp.dot(inner_ref[0], down[0][:, where], preferred_element_type=f32)
        value += jnp.dot(inner_ref[1], down[1][:, where], preferred_element_type=f32)
        if residual:
            value = hid_ref[:, where] + tiled(mod_ref[0, :, where], x_ref.shape[0]) * value
        out_ref[:, where] = value.astype(out_ref.dtype)


def feed_forward(x, ups, downs, extra=()):
    rows, width = x.shape
    units = ups[0].shape[0]
    return pl.pallas_call(
        functools.partial(ffn_kernel, bool(extra)),
        out_shape=jax.ShapeDtypeStruct(x.shape, bf16 if extra else f32),
        in_specs=in_vmem(5 + len(extra)),
        out_specs=in_vmem(1)[0],
        scratch_shapes=[pltpu.VMEM((2, rows, units), bf16)],
        compiler_params=params(8),
        cost_estimate=cost(8 * rows * width * units, 8 * units * width),
        name="feed_forward",
    )(x, *extra, *ups, *downs)


def head_kernel(steps_ref, table_ref, ffn_ref, hid_ref, w_ref, out_ref, out16_ref):
    gate = rows_of_frames(steps_ref, table_ref, 0)
    rows = ffn_ref.shape[0]
    hidden = hid_ref[...].astype(f32) + tiled(gate, rows) * ffn_ref[...]
    value = normalized(hidden).astype(bf16)
    raw = lax.dot_general(value, w_ref[...], NT, preferred_element_type=f32)
    out_ref[...] = raw
    out16_ref[...] = raw.astype(bf16)


def head(steps, table, ffn, hidden, w_head_t):
    shape = (ffn.shape[0], w_head_t.shape[0])
    return pl.pallas_call(
        head_kernel,
        grid=(1,),
        out_shape=[jax.ShapeDtypeStruct(shape, f32), jax.ShapeDtypeStruct(shape, bf16)],
        in_specs=[
            pl.BlockSpec(memory_space=pltpu.SMEM),
            pl.BlockSpec((1,) + table.shape[1:], lambda i: (5, 0, 0)),
        ]
        + in_vmem(3),
        out_specs=in_vmem(2),
        compiler_params=params(8),
        name="head",
    )(steps, table, ffn, hidden, w_head_t)


def noise_level(step_index):
    fraction = 1.0 - step_index.astype(f32) / STEPS
    return shift_factor * fraction / (1.0 + (shift_factor - 1.0) * fraction)


def join_kernel(windows, frames, steps_ref, lat_ref, raw_ref, before_ref, after_ref, vel_ref, next_ref):
    real, channels = lat_ref.shape
    shift = frames - INTERSECTION
    window = lax.axis_index("win")
    frame = lax.broadcasted_iota(jnp.int32, (real, 1), 0) % frames
    steps = jnp.zeros((real, 1), jnp.int32)
    for f in range(frames):
        steps = jnp.where(frame == f, steps_ref[0, f], steps)
    place = frame.astype(f32)
    left = 1.0 - (place + 1.0) / (INTERSECTION + 1.0)
    left = jnp.where((frame < INTERSECTION) & (window > 0), left, 0.0)
    right = 1.0 - (frames - place) / (INTERSECTION + 1.0)
    right = jnp.where((frame >= shift) & (window < windows - 1), right, 0.0)
    none = jnp.zeros((shift, channels), f32)
    before = before_ref[...].astype(f32)
    after = after_ref[...].astype(f32)
    from_left = jnp.concatenate([before[shift:real], none], axis=0)
    from_right = jnp.concatenate([none, after[: real - shift]], axis=0)
    own = 1.0 - left - right
    velocity = own * raw_ref[:real, :] + left * from_left + right * from_right
    vel_ref[...] = velocity
    next_ref[...] = lat_ref[...] + (noise_level(steps + 1) - noise_level(steps)) * velocity


def join(windows, frames, steps, lat, raw, before, after):
    return pl.pallas_call(
        functools.partial(join_kernel, windows, frames),
        out_shape=[jax.ShapeDtypeStruct(lat.shape, f32)] * 2,
        in_specs=[pl.BlockSpec(memory_space=pltpu.SMEM)] + in_vmem(4),
        out_specs=in_vmem(2),
        compiler_params=params(8),
        name="join",
    )(steps, lat, raw, before, after)


def body(latent, frame_steps, mod_table, w_patch, w_qkv, w_out, w_ff1, w_ff2, w_head):
    _, patches, frames, channels = latent.shape
    windows = lax.axis_size("win")
    devices = windows * lax.axis_size("seq")
    real = patches * frames
    rows = -(-real // 16) * 16
    heads = w_out.shape[0] // HEAD_DIM

    def send(value, target):
        return lax.ppermute(value, AXES, moves(devices, target))

    flat = latent.reshape(real, channels)
    lat = flat.astype(bf16)
    lat = jnp.concatenate([lat, lat[real - frames : real - frames + rows - real]], axis=0)
    lat = jnp.concatenate([lat[: rows // 2], lat[rows // 2 :]], axis=1)
    lat_sib = send(lat, to_sibling)
    lat_chip = send(lat, to_chip)
    lat_cross = send(lat, to_cross)

    table = jnp.transpose(mod_table, (1, 0, 2))
    first_mods, second_mods, last_mods = modulation_rows(frame_steps, table)

    up = w_ff1.T
    lat_sib, lat_chip, lat_cross, steps_near, up_near, out_near = barrier(
        (lat_sib, lat_chip, lat_cross, frame_steps, up, w_out)
    )
    out_chip = send(out_near, to_partner)
    up_sib = send(up_near, to_sibling)

    scale = HEAD_DIM**-0.5 * 1.4426950408889634
    query_own, query_sib, keys, values = project(
        [lat, lat_sib], first_mods, w_patch, w_qkv, real, scale
    )
    query_chip, keys, values = project(
        [lat_chip], first_mods, w_patch, w_qkv, real, scale, (keys, values)
    )
    query_cross, keys, values = project(
        [lat_cross], first_mods, w_patch, w_qkv, real, scale, (keys, values), (out_chip,)
    )
    keys, up_sib, down_near, out_near, steps_near = barrier(
        (keys, up_sib, w_ff2, w_out, frame_steps)
    )
    steps_partner = send(steps_near, to_partner)
    out_sib = send(out_near, to_sibling)
    down_sib = send(down_near, to_sibling)

    (att_cross,) = attend([query_cross], keys, values)
    got_cross = send(att_cross, to_cross)
    (att_chip,) = attend([query_chip], keys, values)
    out_cross = send(out_chip, to_sibling)
    got_chip = send(att_chip, to_chip)
    att_sib, att_own = attend([query_sib, query_own], keys, values, (steps_partner,))
    got_sib = send(att_sib, to_sibling)

    hidden1, normed2 = output(
        (att_own, got_sib, got_chip, got_cross),
        (w_out, out_sib, out_chip, out_cross),
        lat,
        second_mods,
        w_patch,
    )
    normed_partner = send(normed2, to_partner)
    ups, downs = (up, up_sib), (w_ff2, down_sib)
    hidden_near = feed_forward(normed2, ups, downs, (hidden1, last_mods))
    hidden_partner = send(hidden_near, to_partner)
    ffn_partner = feed_forward(normed_partner, ups, downs)
    raw_partner, raw16 = head(steps_partner, table, ffn_partner, hidden_partner, w_head.T)

    owner = [to for _, to in moves(devices, to_partner)]
    up_next = [(i, owner[i] + 4) for i in range(devices) if owner[i] + 4 < devices]
    down_next = [(i, owner[i] - 4) for i in range(devices) if owner[i] - 4 >= 0]
    before = lax.ppermute(raw16, AXES, up_next)
    after = lax.ppermute(raw16, AXES, down_next)
    raw = send(raw_partner, to_partner)
    velocity, latent_next = join(windows, frames, frame_steps, flat, raw, before, after)
    shape = latent.shape
    return velocity.reshape(shape), latent_next.reshape(shape)


def solution(mesh):
    in_specs = (
        P("win", "seq", None, None),
        P("win", None),
        P(),
        P(),
        P(None, "seq"),
        P("seq", None),
        P(None, "seq"),
        P("seq", None),
        P(),
    )
    out_specs = (P("win", "seq", None, None), P("win", "seq", None, None))
    return jax.shard_map(body, mesh=mesh, in_specs=in_specs, out_specs=out_specs, check_vma=False)
```

```python
import functools

import jax
import jax.numpy as jnp
from jax import lax
from jax.experimental import pallas as pl
from jax.experimental.pallas import tpu as pltpu
from jax.sharding import PartitionSpec as P

HEAD_DIM = 128
INTERSECTION = 2
STEPS = 50
PERIOD = 40

epsilon = 1e-06
shift_factor = 5.0
bf16 = jnp.bfloat16
f32 = jnp.float32
AXES = ("win", "seq")
NT = (((1,), (1,)), ((), ()))
MIB = 2**20


def place_of(index):
    win, seq = divmod(index, 4)
    y, rest = divmod(win, 8)
    x_hi, z = divmod(rest, 4)
    x_lo, core = divmod(seq, 2)
    return x_hi * 2 + x_lo, y, z, core


def index_of(x, y, z, core):
    x_hi, x_lo = divmod(x % 4, 2)
    return ((y * 2 + x_hi) * 4 + z) * 4 + x_lo * 2 + core


def moves(count, target):
    return [(i, index_of(*target(*place_of(i)))) for i in range(count)]


def to_sibling(x, y, z, core):
    return x, y, z, 1 - core


def to_chip(x, y, z, core):
    return x ^ 1, y, z, core


def to_cross(x, y, z, core):
    return x ^ 1, y, z, 1 - core


def to_far(x, y, z, core):
    return (x - 1 if x % 2 == 0 else x + 1), y, z, core


def to_partner(x, y, z, core):
    return to_chip(x, y, z, core) if core == 0 else to_far(x, y, z, core)


barrier = lax.optimization_barrier


def row_groups(rows):
    return [(start, min(2 * PERIOD, rows - start)) for start in range(0, rows, 2 * PERIOD)]


def tiled(pattern, rows):
    pieces = [pattern] * (rows // PERIOD)
    if rows % PERIOD:
        pieces.append(pattern[: rows % PERIOD])
    return jnp.concatenate(pieces, axis=0) if len(pieces) > 1 else pieces[0]


def normalized(values):
    centered = values - jnp.mean(values, axis=-1, keepdims=True)
    variance = jnp.mean(centered * centered, axis=-1, keepdims=True)
    return centered * lax.rsqrt(variance + epsilon)


def gelu(x):
    inside = x * (0.7978845608028654 + 0.035677408136300125 * (x * x))
    half = 0.5 * x
    return half + half * jnp.tanh(inside)


def in_vmem(count):
    return [pl.BlockSpec(memory_space=pltpu.VMEM)] * count


def params(size):
    return pltpu.CompilerParams(vmem_limit_bytes=size * MIB)


def anywhere(count):
    return [pl.BlockSpec(memory_space=pl.ANY)] * count


def cost(flops, size):
    return pl.CostEstimate(flops=int(flops), bytes_accessed=int(size), transcendentals=0)


def rows_of_frames(steps_ref, table_ref, j):
    frame = lax.broadcasted_iota(jnp.int32, (8, 1), 0)
    vectors = [table_ref[j, pl.ds(steps_ref[0, f], 1), :] for f in range(5)]
    pieces = []
    for part in range(5):
        at = (frame + 8 * part) % 5
        tile = jnp.broadcast_to(vectors[0], (8, vectors[0].shape[1]))
        for f in range(1, 5):
            tile = jnp.where(at == f, vectors[f], tile)
        pieces.append(tile)
    return jnp.concatenate(pieces, axis=0)


def modulation_kernel(steps_ref, table_ref, first_ref, second_ref, last_ref):
    for j in range(6):
        out_ref, at = ((first_ref, j), (second_ref, j - 2), (last_ref, 0))[(j > 1) + (j > 4)]
        out_ref[at] = rows_of_frames(steps_ref, table_ref, j)


def modulation_rows(steps, table):
    return pl.pallas_call(
        modulation_kernel,
        out_shape=[jax.ShapeDtypeStruct((n, PERIOD, table.shape[2]), f32) for n in (2, 3, 1)],
        in_specs=[pl.BlockSpec(memory_space=pltpu.SMEM)] + in_vmem(1),
        out_specs=in_vmem(3),
        compiler_params=params(8),
        name="modulation",
    )(steps, table)


def project_block(lat_ref, mod_ref, w_patch_ref, w_qkv_ref, normed_ref, store):
    half, lanes = lat_ref.shape
    channels = lanes // 2
    for side in range(2):
        lat = lat_ref[:, side * channels : (side + 1) * channels]
        embed = jnp.dot(lat, w_patch_ref[...], preferred_element_type=f32)
        normed_ref[side * half : (side + 1) * half, :] = embed
    normed = []
    for start, count in row_groups(2 * half):
        value = normalized(normed_ref[start : start + count, :])
        value = value * (1.0 + tiled(mod_ref[1], count)) + tiled(mod_ref[0], count)
        normed.append(value.astype(bf16))
    normed = jnp.concatenate(normed, axis=0)
    columns = w_qkv_ref.shape[1]
    for c in range(0, columns, 256):
        end = min(c + 256, columns)
        part = jnp.dot(normed, w_qkv_ref[:, c:end], preferred_element_type=f32)
        for d in range(c, end, HEAD_DIM):
            h, j = divmod(d // HEAD_DIM, 3)
            store(h, j, part[:, d - c : d - c + HEAD_DIM])


def store_block(b, real, scale, query_ref, key_ref, value_ref):
    rows = query_ref.shape[0]
    where = slice(b * rows, (b + 1) * rows)

    def store(h, j, piece):
        if j == 0:
            query_ref[:, h * HEAD_DIM : (h + 1) * HEAD_DIM] = (piece * scale).astype(bf16)
        elif j == 1:
            key_ref[h, where, :] = piece.astype(bf16)
        else:
            at = lax.broadcasted_iota(jnp.int32, piece.shape, 0) < real
            value_ref[h, where, :HEAD_DIM] = jnp.where(at, piece, 0.0).astype(bf16)
            value_ref[h, where, HEAD_DIM:] = jnp.where(at, 1.0, 0.0).astype(bf16)

    return store


def project_kernel(blocks, placed, real, scale, after, *refs):
    lat_refs = refs[:blocks]
    mod_ref, w_patch_ref, w_qkv_ref = refs[blocks : blocks + 3]
    refs = refs[blocks + 3 :]
    if placed:
        key_in, value_in = refs[:2]
        refs = refs[2:]
    refs = refs[after:]
    query_refs = refs[:blocks]
    key_ref, value_ref, embed_ref = refs[blocks:]
    rows = query_refs[0].shape[0]
    if placed:
        key_ref[:, : placed * rows, :] = key_in[...]
        value_ref[:, : placed * rows, :] = value_in[...]
    for b in range(blocks):
        store = store_block(placed + b, real, scale, query_refs[b], key_ref, value_ref)
        project_block(lat_refs[b], mod_ref, w_patch_ref, w_qkv_ref, embed_ref.at[b], store)


def project(lats, mods, w_patch, w_qkv, real, scale, before=(), after=()):
    blocks = len(lats)
    rows = 2 * lats[0].shape[0]
    width, columns = w_qkv.shape
    heads = columns // (3 * HEAD_DIM)
    placed = before[0].shape[1] // rows if before else 0
    tokens = (placed + blocks) * rows
    return pl.pallas_call(
        functools.partial(project_kernel, blocks, placed, real, scale, len(after)),
        out_shape=[jax.ShapeDtypeStruct((rows, heads * HEAD_DIM), bf16)] * blocks
        + [
            jax.ShapeDtypeStruct((heads, tokens, HEAD_DIM), bf16),
            jax.ShapeDtypeStruct((heads, tokens, 2 * HEAD_DIM), bf16),
        ],
        in_specs=in_vmem(blocks + 3 + len(before)) + anywhere(len(after)),
        out_specs=in_vmem(blocks + 2),
        scratch_shapes=[pltpu.VMEM((blocks, rows, width), f32)],
        compiler_params=params(8),
        cost_estimate=cost(rows, rows),
        name="project",
    )(*lats, mods, w_patch, w_qkv, *before, *after)


def attend_kernel(blocks, after, *refs):
    query_refs = refs[:blocks]
    key_ref, value_ref = refs[blocks : blocks + 2]
    out_refs = refs[blocks + 2 + after :]
    for query_ref, out_ref in zip(query_refs, out_refs):
        for h in range(key_ref.shape[0]):
            columns = slice(h * HEAD_DIM, (h + 1) * HEAD_DIM)
            query = query_ref[:, columns]
            scores = lax.dot_general(query, key_ref[h], NT, preferred_element_type=f32)
            top = jnp.max(scores, axis=1, keepdims=True)
            weights = jnp.exp2(scores - top).astype(bf16)
            both = jnp.dot(weights, value_ref[h], preferred_element_type=f32)
            out_ref[:, columns] = (both[:, :HEAD_DIM] / both[:, HEAD_DIM:]).astype(bf16)


def attend(queries, keys, values, after=()):
    blocks = len(queries)
    rows, width = queries[0].shape
    return pl.pallas_call(
        functools.partial(attend_kernel, blocks, len(after)),
        out_shape=[jax.ShapeDtypeStruct((rows, width), bf16)] * blocks,
        in_specs=in_vmem(blocks + 2) + anywhere(len(after)),
        out_specs=in_vmem(blocks),
        compiler_params=params(8),
        cost_estimate=cost(16 * blocks * rows * width * 4 * rows, 2**20),
        name="attend",
    )(*queries, keys, values, *after)


def output_kernel(a0, a1, a2, a3, w0, w1, w2, w3, lat_ref, mod_ref, w_patch_ref, hid_ref, norm_ref):
    attended = jnp.concatenate([a[...] for a in (a0, a1, a2, a3)], axis=1)
    width = hid_ref.shape[1]
    for c in range(0, width, 256):
        where = slice(c, c + 256)
        weight = jnp.concatenate([w[:, where] for w in (w0, w1, w2, w3)], axis=0)
        total = jnp.dot(attended, weight, preferred_element_type=f32)
        channels = lat_ref.shape[1] // 2
        lat = jnp.concatenate([lat_ref[:, :channels], lat_ref[:, channels:]], axis=0)
        embed = jnp.dot(lat, w_patch_ref[:, where], preferred_element_type=f32)
        gate = tiled(mod_ref[0, :, where], hid_ref.shape[0])
        hid_ref[:, where] = embed + gate * total
    for start, count in row_groups(hid_ref.shape[0]):
        rows = slice(start, start + count)
        value = normalized(hid_ref[rows, :]) * (1.0 + tiled(mod_ref[2], count))
        norm_ref[rows, :] = (value + tiled(mod_ref[1], count)).astype(bf16)


def output(attended, weights, lat, mods, w_patch):
    shape = (2 * lat.shape[0], w_patch.shape[1])
    return pl.pallas_call(
        output_kernel,
        out_shape=[jax.ShapeDtypeStruct(shape, f32), jax.ShapeDtypeStruct(shape, bf16)],
        in_specs=in_vmem(11),
        out_specs=in_vmem(2),
        compiler_params=params(8),
        cost_estimate=cost(2 * shape[0] * shape[1] ** 2, 2 * shape[1] ** 2),
        name="output",
    )(*attended, *weights, lat, mods, w_patch)


UNITS = 512
COLUMNS = 256


def ffn_kernel(residual, *refs):
    if residual:
        x_ref, hid_ref, mod_ref = refs[:3]
        refs = refs[3:]
    else:
        x_ref = refs[0]
        refs = refs[1:]
    up = refs[0:2]
    down = refs[2:4]
    out_ref, inner_ref = refs[4:]
    units = up[0].shape[0]
    width = x_ref.shape[1]
    for half in range(2):
        for start in range(0, units, UNITS):
            end = min(start + UNITS, units)
            weight = up[half][start:end, :]
            inner = lax.dot_general(x_ref[...], weight, NT, preferred_element_type=f32)
            inner_ref[half, :, start:end] = gelu(inner).astype(bf16)
    for start in range(0, width, COLUMNS):
        where = slice(start, start + COLUMNS)
        value = jnp.dot(inner_ref[0], down[0][:, where], preferred_element_type=f32)
        value += jnp.dot(inner_ref[1], down[1][:, where], preferred_element_type=f32)
        if residual:
            value = hid_ref[:, where] + tiled(mod_ref[0, :, where], x_ref.shape[0]) * value
        out_ref[:, where] = value.astype(out_ref.dtype)


def feed_forward(x, ups, downs, extra=()):
    rows, width = x.shape
    units = ups[0].shape[0]
    return pl.pallas_call(
        functools.partial(ffn_kernel, bool(extra)),
        out_shape=jax.ShapeDtypeStruct(x.shape, bf16 if extra else f32),
        in_specs=in_vmem(5 + len(extra)),
        out_specs=in_vmem(1)[0],
        scratch_shapes=[pltpu.VMEM((2, rows, units), bf16)],
        compiler_params=params(8),
        cost_estimate=cost(8 * rows * width * units, 8 * units * width),
        name="feed_forward",
    )(x, *extra, *ups, *downs)


def head_kernel(steps_ref, table_ref, ffn_ref, hid_ref, w_ref, out_ref, out16_ref):
    gate = rows_of_frames(steps_ref, table_ref, 0)
    rows = ffn_ref.shape[0]
    hidden = hid_ref[...].astype(f32) + tiled(gate, rows) * ffn_ref[...]
    value = normalized(hidden).astype(bf16)
    raw = lax.dot_general(value, w_ref[...], NT, preferred_element_type=f32)
    out_ref[...] = raw
    out16_ref[...] = raw.astype(bf16)


def head(steps, table, ffn, hidden, w_head_t):
    shape = (ffn.shape[0], w_head_t.shape[0])
    return pl.pallas_call(
        head_kernel,
        grid=(1,),
        out_shape=[jax.ShapeDtypeStruct(shape, f32), jax.ShapeDtypeStruct(shape, bf16)],
        in_specs=[
            pl.BlockSpec(memory_space=pltpu.SMEM),
            pl.BlockSpec((1,) + table.shape[1:], lambda i: (5, 0, 0)),
        ]
        + in_vmem(3),
        out_specs=in_vmem(2),
        compiler_params=params(8),
        name="head",
    )(steps, table, ffn, hidden, w_head_t)


def noise_level(step_index):
    fraction = 1.0 - step_index.astype(f32) / STEPS
    return shift_factor * fraction / (1.0 + (shift_factor - 1.0) * fraction)


def join_kernel(windows, frames, steps_ref, lat_ref, raw_ref, before_ref, after_ref, vel_ref, next_ref):
    real, channels = lat_ref.shape
    shift = frames - INTERSECTION
    window = lax.axis_index("win")
    frame = lax.broadcasted_iota(jnp.int32, (real, 1), 0) % frames
    steps = jnp.zeros((real, 1), jnp.int32)
    for f in range(frames):
        steps = jnp.where(frame == f, steps_ref[0, f], steps)
    place = frame.astype(f32)
    left = 1.0 - (place + 1.0) / (INTERSECTION + 1.0)
    left = jnp.where((frame < INTERSECTION) & (window > 0), left, 0.0)
    right = 1.0 - (frames - place) / (INTERSECTION + 1.0)
    right = jnp.where((frame >= shift) & (window < windows - 1), right, 0.0)
    none = jnp.zeros((shift, channels), f32)
    before = before_ref[...].astype(f32)
    after = after_ref[...].astype(f32)
    from_left = jnp.concatenate([before[shift:real], none], axis=0)
    from_right = jnp.concatenate([none, after[: real - shift]], axis=0)
    own = 1.0 - left - right
    velocity = own * raw_ref[:real, :] + left * from_left + right * from_right
    vel_ref[...] = velocity
    next_ref[...] = lat_ref[...] + (noise_level(steps + 1) - noise_level(steps)) * velocity


def join(windows, frames, steps, lat, raw, before, after):
    return pl.pallas_call(
        functools.partial(join_kernel, windows, frames),
        out_shape=[jax.ShapeDtypeStruct(lat.shape, f32)] * 2,
        in_specs=[pl.BlockSpec(memory_space=pltpu.SMEM)] + in_vmem(4),
        out_specs=in_vmem(2),
        compiler_params=params(8),
        name="join",
    )(steps, lat, raw, before, after)


def body(latent, frame_steps, mod_table, w_patch, w_qkv, w_out, w_ff1, w_ff2, w_head):
    _, patches, frames, channels = latent.shape
    windows = lax.axis_size("win")
    devices = windows * lax.axis_size("seq")
    real = patches * frames
    rows = -(-real // 16) * 16
    heads = w_out.shape[0] // HEAD_DIM

    def send(value, target):
        return lax.ppermute(value, AXES, moves(devices, target))

    flat = latent.reshape(real, channels)
    lat = flat.astype(bf16)
    lat = jnp.concatenate([lat, lat[real - frames : real - frames + rows - real]], axis=0)
    lat = jnp.concatenate([lat[: rows // 2], lat[rows // 2 :]], axis=1)
    lat_sib = send(lat, to_sibling)
    lat_chip = send(lat, to_chip)
    lat_cross = send(lat, to_cross)

    table = jnp.transpose(mod_table, (1, 0, 2))
    first_mods, second_mods, last_mods = modulation_rows(frame_steps, table)

    up = w_ff1.T
    lat_sib, lat_chip, lat_cross, up_near, down_near, out_near = barrier(
        (lat_sib, lat_chip, lat_cross, up, w_ff2, w_out)
    )
    out_chip = send(out_near, to_partner)
    up_sib = send(up_near, to_sibling)
    down_sib = send(down_near, to_sibling)

    scale = HEAD_DIM**-0.5 * 1.4426950408889634
    query_own, query_sib, keys, values = project(
        [lat, lat_sib], first_mods, w_patch, w_qkv, real, scale
    )
    query_chip, query_cross, keys, values = project(
        [lat_chip, lat_cross], first_mods, w_patch, w_qkv, real, scale, (keys, values)
    )
    (att_cross,) = attend([query_cross], keys, values, (up_sib,))
    got_cross = send(att_cross, to_cross)
    (att_chip,) = attend([query_chip], keys, values)
    got_chip = send(att_chip, to_chip)
    (att_sib,) = attend([query_sib], keys, values, (att_cross, att_chip))
    (att_own,) = attend([query_own], keys, values, (att_sib, down_sib))
    out_chip, _, out_near = barrier((out_chip, att_chip, w_out))
    _, steps_near = barrier((att_own, frame_steps))
    got_sib = send(att_sib, to_sibling)
    out_cross = send(out_chip, to_sibling)
    out_sib = send(out_near, to_sibling)
    steps_partner = send(steps_near, to_partner)

    hidden1, normed2 = output(
        (att_own, got_sib, got_chip, got_cross),
        (w_out, out_sib, out_chip, out_cross),
        lat,
        second_mods,
        w_patch,
    )
    normed_partner = send(normed2, to_partner)
    ups, downs = (up, up_sib), (w_ff2, down_sib)
    hidden_near = feed_forward(normed2, ups, downs, (hidden1, last_mods))
    hidden_partner = send(hidden_near, to_partner)
    ffn_partner = feed_forward(normed_partner, ups, downs)
    raw_partner, raw16 = head(steps_partner, table, ffn_partner, hidden_partner, w_head.T)

    owner = [to for _, to in moves(devices, to_partner)]
    up_next = [(i, owner[i] + 4) for i in range(devices) if owner[i] + 4 < devices]
    down_next = [(i, owner[i] - 4) for i in range(devices) if owner[i] - 4 >= 0]
    before = lax.ppermute(raw16, AXES, up_next)
    after = lax.ppermute(raw16, AXES, down_next)
    raw = send(raw_partner, to_partner)
    velocity, latent_next = join(windows, frames, frame_steps, flat, raw, before, after)
    shape = latent.shape
    return velocity.reshape(shape), latent_next.reshape(shape)


def solution(mesh):
    in_specs = (
        P("win", "seq", None, None),
        P("win", None),
        P(),
        P(),
        P(None, "seq"),
        P("seq", None),
        P(None, "seq"),
        P("seq", None),
        P(),
    )
    out_specs = (P("win", "seq", None, None), P("win", "seq", None, None))
    return jax.shard_map(body, mesh=mesh, in_specs=in_specs, out_specs=out_specs, check_vma=False)
```

```python
import functools

import jax
import jax.numpy as jnp
from jax import lax
from jax.experimental import pallas as pl
from jax.experimental.pallas import tpu as pltpu
from jax.sharding import PartitionSpec as P

HEAD_DIM = 128
INTERSECTION = 2
STEPS = 50
PERIOD = 40

epsilon = 1e-06
shift_factor = 5.0
bf16 = jnp.bfloat16
f32 = jnp.float32
AXES = ("win", "seq")
NT = (((1,), (1,)), ((), ()))
MIB = 2**20


def place_of(index):
    win, seq = divmod(index, 4)
    y, rest = divmod(win, 8)
    x_hi, z = divmod(rest, 4)
    x_lo, core = divmod(seq, 2)
    return x_hi * 2 + x_lo, y, z, core


def index_of(x, y, z, core):
    x_hi, x_lo = divmod(x % 4, 2)
    return ((y * 2 + x_hi) * 4 + z) * 4 + x_lo * 2 + core


def moves(count, target):
    return [(i, index_of(*target(*place_of(i)))) for i in range(count)]


def to_sibling(x, y, z, core):
    return x, y, z, 1 - core


def to_chip(x, y, z, core):
    return x ^ 1, y, z, core


def to_cross(x, y, z, core):
    return x ^ 1, y, z, 1 - core


def to_far(x, y, z, core):
    return (x - 1 if x % 2 == 0 else x + 1), y, z, core


def to_partner(x, y, z, core):
    return to_chip(x, y, z, core) if core == 0 else to_far(x, y, z, core)


barrier = lax.optimization_barrier


def row_groups(rows):
    return [(start, min(2 * PERIOD, rows - start)) for start in range(0, rows, 2 * PERIOD)]


def tiled(pattern, rows):
    pieces = [pattern] * (rows // PERIOD)
    if rows % PERIOD:
        pieces.append(pattern[: rows % PERIOD])
    return jnp.concatenate(pieces, axis=0) if len(pieces) > 1 else pieces[0]


def normalized(values):
    centered = values - jnp.mean(values, axis=-1, keepdims=True)
    variance = jnp.mean(centered * centered, axis=-1, keepdims=True)
    return centered * lax.rsqrt(variance + epsilon)


def gelu(x):
    inside = x * (0.7978845608028654 + 0.035677408136300125 * (x * x))
    half = 0.5 * x
    return half + half * jnp.tanh(inside)


def in_vmem(count):
    return [pl.BlockSpec(memory_space=pltpu.VMEM)] * count


def params(size):
    return pltpu.CompilerParams(vmem_limit_bytes=size * MIB)


def anywhere(count):
    return [pl.BlockSpec(memory_space=pl.ANY)] * count


def cost(flops, size):
    return pl.CostEstimate(flops=int(flops), bytes_accessed=int(size), transcendentals=0)


def rows_of_frames(steps_ref, table_ref, j):
    frame = lax.broadcasted_iota(jnp.int32, (8, 1), 0)
    vectors = [table_ref[j, pl.ds(steps_ref[0, f], 1), :] for f in range(5)]
    pieces = []
    for part in range(5):
        at = (frame + 8 * part) % 5
        tile = jnp.broadcast_to(vectors[0], (8, vectors[0].shape[1]))
        for f in range(1, 5):
            tile = jnp.where(at == f, vectors[f], tile)
        pieces.append(tile)
    return jnp.concatenate(pieces, axis=0)


def modulation_kernel(steps_ref, table_ref, first_ref, second_ref, last_ref):
    for j in range(6):
        out_ref, at = ((first_ref, j), (second_ref, j - 2), (last_ref, 0))[(j > 1) + (j > 4)]
        out_ref[at] = rows_of_frames(steps_ref, table_ref, j)


def modulation_rows(steps, table):
    return pl.pallas_call(
        modulation_kernel,
        out_shape=[jax.ShapeDtypeStruct((n, PERIOD, table.shape[2]), f32) for n in (2, 3, 1)],
        in_specs=[pl.BlockSpec(memory_space=pltpu.SMEM)] + in_vmem(1),
        out_specs=in_vmem(3),
        compiler_params=params(8),
        name="modulation",
    )(steps, table)


def pack_kernel(frames, lat_ref, out_ref):
    real = lat_ref.shape[0]
    half = out_ref.shape[0]
    lat = lat_ref[:, 0, :]
    lat = jnp.concatenate([lat, lat[real - frames : 2 * half - frames]], axis=0)
    out_ref[...] = jnp.concatenate([lat[:half], lat[half:]], axis=1).astype(bf16)


def pack(lat, rows, frames):
    return pl.pallas_call(
        functools.partial(pack_kernel, frames),
        out_shape=jax.ShapeDtypeStruct((rows // 2, 2 * lat.shape[2]), bf16),
        in_specs=in_vmem(1),
        out_specs=in_vmem(1)[0],
        compiler_params=params(8),
        name="pack",
    )(lat)


def project_block(lat_ref, mod_ref, w_patch_ref, w_qkv_ref, normed_ref, store):
    half, lanes = lat_ref.shape
    channels = lanes // 2
    for side in range(2):
        lat = lat_ref[:, side * channels : (side + 1) * channels]
        embed = jnp.dot(lat, w_patch_ref[...], preferred_element_type=f32)
        normed_ref[side * half : (side + 1) * half, :] = embed
    normed = []
    for start, count in row_groups(2 * half):
        value = normalized(normed_ref[start : start + count, :])
        value = value * (1.0 + tiled(mod_ref[1], count)) + tiled(mod_ref[0], count)
        normed.append(value.astype(bf16))
    normed = jnp.concatenate(normed, axis=0)
    columns = w_qkv_ref.shape[1]
    for c in range(0, columns, 256):
        end = min(c + 256, columns)
        part = jnp.dot(normed, w_qkv_ref[:, c:end], preferred_element_type=f32)
        for d in range(c, end, HEAD_DIM):
            h, j = divmod(d // HEAD_DIM, 3)
            store(h, j, part[:, d - c : d - c + HEAD_DIM])


def store_block(b, real, scale, query_ref, key_ref, value_ref):
    rows = query_ref.shape[0]
    where = slice(b * rows, (b + 1) * rows)

    def store(h, j, piece):
        if j == 0:
            query_ref[:, h * HEAD_DIM : (h + 1) * HEAD_DIM] = (piece * scale).astype(bf16)
        elif j == 1:
            key_ref[h, where, :] = piece.astype(bf16)
        else:
            at = lax.broadcasted_iota(jnp.int32, piece.shape, 0) < real
            value_ref[h, where, :HEAD_DIM] = jnp.where(at, piece, 0.0).astype(bf16)
            value_ref[h, where, HEAD_DIM:] = jnp.where(at, 1.0, 0.0).astype(bf16)

    return store


def project_kernel(blocks, placed, real, scale, after, *refs):
    lat_refs = refs[:blocks]
    mod_ref, w_patch_ref, w_qkv_ref = refs[blocks : blocks + 3]
    refs = refs[blocks + 3 :]
    if placed:
        key_in, value_in = refs[:2]
        refs = refs[2:]
    refs = refs[after:]
    query_refs = refs[:blocks]
    key_ref, value_ref, embed_ref = refs[blocks:]
    rows = query_refs[0].shape[0]
    if placed:
        key_ref[:, : placed * rows, :] = key_in[...]
        value_ref[:, : placed * rows, :] = value_in[...]
    for b in range(blocks):
        store = store_block(placed + b, real, scale, query_refs[b], key_ref, value_ref)
        project_block(lat_refs[b], mod_ref, w_patch_ref, w_qkv_ref, embed_ref.at[b], store)


def project(lats, mods, w_patch, w_qkv, real, scale, before=(), after=()):
    blocks = len(lats)
    rows = 2 * lats[0].shape[0]
    width, columns = w_qkv.shape
    heads = columns // (3 * HEAD_DIM)
    placed = before[0].shape[1] // rows if before else 0
    tokens = (placed + blocks) * rows
    return pl.pallas_call(
        functools.partial(project_kernel, blocks, placed, real, scale, len(after)),
        out_shape=[jax.ShapeDtypeStruct((rows, heads * HEAD_DIM), bf16)] * blocks
        + [
            jax.ShapeDtypeStruct((heads, tokens, HEAD_DIM), bf16),
            jax.ShapeDtypeStruct((heads, tokens, 2 * HEAD_DIM), bf16),
        ],
        in_specs=in_vmem(blocks + 3 + len(before)) + anywhere(len(after)),
        out_specs=in_vmem(blocks + 2),
        scratch_shapes=[pltpu.VMEM((blocks, rows, width), f32)],
        compiler_params=params(8),
        cost_estimate=cost(rows, rows),
        name="project",
    )(*lats, mods, w_patch, w_qkv, *before, *after)


def attend_kernel(blocks, after, *refs):
    query_refs = refs[:blocks]
    key_ref, value_ref = refs[blocks : blocks + 2]
    out_refs = refs[blocks + 2 + after :]
    for query_ref, out_ref in zip(query_refs, out_refs):
        for h in range(key_ref.shape[0]):
            columns = slice(h * HEAD_DIM, (h + 1) * HEAD_DIM)
            query = query_ref[:, columns]
            scores = lax.dot_general(query, key_ref[h], NT, preferred_element_type=f32)
            top = jnp.max(scores, axis=1, keepdims=True)
            weights = jnp.exp2(scores - top).astype(bf16)
            both = jnp.dot(weights, value_ref[h], preferred_element_type=f32)
            out_ref[:, columns] = (both[:, :HEAD_DIM] / both[:, HEAD_DIM:]).astype(bf16)


def attend(queries, keys, values, after=()):
    blocks = len(queries)
    rows, width = queries[0].shape
    return pl.pallas_call(
        functools.partial(attend_kernel, blocks, len(after)),
        out_shape=[jax.ShapeDtypeStruct((rows, width), bf16)] * blocks,
        in_specs=in_vmem(blocks + 2) + anywhere(len(after)),
        out_specs=in_vmem(blocks),
        compiler_params=params(8),
        cost_estimate=cost(16 * blocks * rows * width * 4 * rows, 2**20),
        name="attend",
    )(*queries, keys, values, *after)


def output_kernel(a0, a1, a2, a3, w0, w1, w2, w3, lat_ref, mod_ref, w_patch_ref, hid_ref, norm_ref):
    attended = jnp.concatenate([a[...] for a in (a0, a1, a2, a3)], axis=1)
    width = hid_ref.shape[1]
    for c in range(0, width, 256):
        where = slice(c, c + 256)
        weight = jnp.concatenate([w[:, where] for w in (w0, w1, w2, w3)], axis=0)
        total = jnp.dot(attended, weight, preferred_element_type=f32)
        channels = lat_ref.shape[1] // 2
        embed = [
            jnp.dot(lat, w_patch_ref[:, where], preferred_element_type=f32)
            for lat in (lat_ref[:, :channels], lat_ref[:, channels:])
        ]
        embed = jnp.concatenate(embed, axis=0)
        gate = tiled(mod_ref[0, :, where], hid_ref.shape[0])
        hid_ref[:, where] = embed + gate * total
    for start, count in row_groups(hid_ref.shape[0]):
        rows = slice(start, start + count)
        value = normalized(hid_ref[rows, :]) * (1.0 + tiled(mod_ref[2], count))
        norm_ref[rows, :] = (value + tiled(mod_ref[1], count)).astype(bf16)


def output(attended, weights, lat, mods, w_patch):
    shape = (2 * lat.shape[0], w_patch.shape[1])
    return pl.pallas_call(
        output_kernel,
        out_shape=[jax.ShapeDtypeStruct(shape, f32), jax.ShapeDtypeStruct(shape, bf16)],
        in_specs=in_vmem(11),
        out_specs=in_vmem(2),
        compiler_params=params(8),
        cost_estimate=cost(2 * shape[0] * shape[1] ** 2, 2 * shape[1] ** 2),
        name="output",
    )(*attended, *weights, lat, mods, w_patch)


UNITS = 512
COLUMNS = 256


def ffn_kernel(residual, *refs):
    if residual:
        x_ref, hid_ref, mod_ref = refs[:3]
        refs = refs[3:]
    else:
        x_ref = refs[0]
        refs = refs[1:]
    up = refs[0:2]
    down = refs[2:4]
    out_ref, inner_ref = refs[4:]
    units = up[0].shape[0]
    width = x_ref.shape[1]
    for half in range(2):
        for start in range(0, units, UNITS):
            end = min(start + UNITS, units)
            weight = up[half][start:end, :]
            inner = lax.dot_general(x_ref[...], weight, NT, preferred_element_type=f32)
            inner_ref[half, :, start:end] = gelu(inner).astype(bf16)
    for start in range(0, width, COLUMNS):
        where = slice(start, start + COLUMNS)
        value = jnp.dot(inner_ref[0], down[0][:, where], preferred_element_type=f32)
        value += jnp.dot(inner_ref[1], down[1][:, where], preferred_element_type=f32)
        if residual:
            value = hid_ref[:, where] + tiled(mod_ref[0, :, where], x_ref.shape[0]) * value
        out_ref[:, where] = value.astype(out_ref.dtype)


def feed_forward(x, ups, downs, extra=()):
    rows, width = x.shape
    units = ups[0].shape[0]
    return pl.pallas_call(
        functools.partial(ffn_kernel, bool(extra)),
        out_shape=jax.ShapeDtypeStruct(x.shape, bf16 if extra else f32),
        in_specs=in_vmem(5 + len(extra)),
        out_specs=in_vmem(1)[0],
        scratch_shapes=[pltpu.VMEM((2, rows, units), bf16)],
        compiler_params=params(8),
        cost_estimate=cost(8 * rows * width * units, 8 * units * width),
        name="feed_forward",
    )(x, *extra, *ups, *downs)


def head_kernel(steps_ref, table_ref, ffn_ref, hid_ref, w_ref, out_ref, out16_ref):
    gate = rows_of_frames(steps_ref, table_ref, 0)
    rows = ffn_ref.shape[0]
    hidden = hid_ref[...].astype(f32) + tiled(gate, rows) * ffn_ref[...]
    value = normalized(hidden).astype(bf16)
    raw = lax.dot_general(value, w_ref[...], NT, preferred_element_type=f32)
    out_ref[...] = raw
    out16_ref[...] = raw.astype(bf16)


def head(steps, table, ffn, hidden, w_head_t):
    shape = (ffn.shape[0], w_head_t.shape[0])
    return pl.pallas_call(
        head_kernel,
        grid=(1,),
        out_shape=[jax.ShapeDtypeStruct(shape, f32), jax.ShapeDtypeStruct(shape, bf16)],
        in_specs=[
            pl.BlockSpec(memory_space=pltpu.SMEM),
            pl.BlockSpec((1,) + table.shape[1:], lambda i: (5, 0, 0)),
        ]
        + in_vmem(3),
        out_specs=in_vmem(2),
        compiler_params=params(8),
        name="head",
    )(steps, table, ffn, hidden, w_head_t)


def noise_level(step_index):
    fraction = 1.0 - step_index.astype(f32) / STEPS
    return shift_factor * fraction / (1.0 + (shift_factor - 1.0) * fraction)


def join_kernel(windows, frames, steps_ref, lat_ref, raw_ref, before_ref, after_ref, vel_ref, next_ref):
    real, _, channels = lat_ref.shape
    shift = frames - INTERSECTION
    window = lax.axis_index("win")
    frame = lax.broadcasted_iota(jnp.int32, (real, 1), 0) % frames
    steps = jnp.zeros((real, 1), jnp.int32)
    for f in range(frames):
        steps = jnp.where(frame == f, steps_ref[0, f], steps)
    place = frame.astype(f32)
    left = 1.0 - (place + 1.0) / (INTERSECTION + 1.0)
    left = jnp.where((frame < INTERSECTION) & (window > 0), left, 0.0)
    right = 1.0 - (frames - place) / (INTERSECTION + 1.0)
    right = jnp.where((frame >= shift) & (window < windows - 1), right, 0.0)
    none = jnp.zeros((shift, channels), f32)
    before = before_ref[...].astype(f32)
    after = after_ref[...].astype(f32)
    from_left = jnp.concatenate([before[shift:real], none], axis=0)
    from_right = jnp.concatenate([none, after[: real - shift]], axis=0)
    own = 1.0 - left - right
    velocity = own * raw_ref[:real, :] + left * from_left + right * from_right
    vel_ref[:, 0, :] = velocity
    step_size = noise_level(steps + 1) - noise_level(steps)
    next_ref[:, 0, :] = lat_ref[:, 0, :] + step_size * velocity


def join(windows, frames, steps, lat, raw, before, after):
    return pl.pallas_call(
        functools.partial(join_kernel, windows, frames),
        out_shape=[jax.ShapeDtypeStruct(lat.shape, f32)] * 2,
        in_specs=[pl.BlockSpec(memory_space=pltpu.SMEM)] + in_vmem(4),
        out_specs=in_vmem(2),
        compiler_params=params(8),
        name="join",
    )(steps, lat, raw, before, after)


def body(latent, frame_steps, mod_table, w_patch, w_qkv, w_out, w_ff1, w_ff2, w_head):
    _, patches, frames, channels = latent.shape
    windows = lax.axis_size("win")
    devices = windows * lax.axis_size("seq")
    real = patches * frames
    rows = -(-real // 16) * 16
    heads = w_out.shape[0] // HEAD_DIM

    def send(value, target):
        return lax.ppermute(value, AXES, moves(devices, target))

    flat = jnp.transpose(latent, (1, 2, 0, 3)).reshape(real, 1, channels)
    lat = pack(flat, rows, frames)
    lat_sib = send(lat, to_sibling)
    lat_chip = send(lat, to_chip)
    lat_cross = send(lat, to_cross)

    table = jnp.transpose(mod_table, (1, 0, 2))
    first_mods, second_mods, last_mods = modulation_rows(frame_steps, table)

    up = w_ff1.T
    lat_sib, lat_chip, lat_cross, first_mods, up_near, down_near, out_near = barrier(
        (lat_sib, lat_chip, lat_cross, first_mods, up, w_ff2, w_out)
    )
    out_chip = send(out_near, to_partner)
    up_sib = send(up_near, to_sibling)
    down_sib = send(down_near, to_sibling)

    scale = HEAD_DIM**-0.5 * 1.4426950408889634
    query_own, query_sib, keys, values = project(
        [lat, lat_sib], first_mods, w_patch, w_qkv, real, scale
    )
    query_chip, query_cross, keys, values = project(
        [lat_chip, lat_cross], first_mods, w_patch, w_qkv, real, scale, (keys, values)
    )
    (att_cross,) = attend([query_cross], keys, values, (up_sib,))
    got_cross = send(att_cross, to_cross)
    (att_chip,) = attend([query_chip], keys, values)
    got_chip = send(att_chip, to_chip)
    (att_sib,) = attend([query_sib], keys, values, (att_cross, att_chip))
    (att_own,) = attend([query_own], keys, values, (att_sib, down_sib))
    out_chip, _, out_near = barrier((out_chip, att_chip, w_out))
    _, steps_near = barrier((att_own, frame_steps))
    got_sib = send(att_sib, to_sibling)
    out_cross = send(out_chip, to_sibling)
    out_sib = send(out_near, to_sibling)
    steps_partner = send(steps_near, to_partner)

    hidden1, normed2 = output(
        (att_own, got_sib, got_chip, got_cross),
        (w_out, out_sib, out_chip, out_cross),
        lat,
        second_mods,
        w_patch,
    )
    normed_partner = send(normed2, to_partner)
    ups, downs = (up, up_sib), (w_ff2, down_sib)
    hidden_near = feed_forward(normed2, ups, downs, (hidden1, last_mods))
    hidden_partner = send(hidden_near, to_partner)
    ffn_partner = feed_forward(normed_partner, ups, downs)
    raw_partner, raw16 = head(steps_partner, table, ffn_partner, hidden_partner, w_head.T)

    owner = [to for _, to in moves(devices, to_partner)]
    up_next = [(i, owner[i] + 4) for i in range(devices) if owner[i] + 4 < devices]
    down_next = [(i, owner[i] - 4) for i in range(devices) if owner[i] - 4 >= 0]
    before = lax.ppermute(raw16, AXES, up_next)
    after = lax.ppermute(raw16, AXES, down_next)
    raw = send(raw_partner, to_partner)
    velocity, latent_next = join(windows, frames, frame_steps, flat, raw, before, after)

    def as_argument(value):
        return jnp.transpose(value.reshape(patches, frames, 1, channels), (2, 0, 1, 3))

    return as_argument(velocity), as_argument(latent_next)


def solution(mesh):
    in_specs = (
        P("win", "seq", None, None),
        P("win", None),
        P(),
        P(),
        P(None, "seq"),
        P("seq", None),
        P(None, "seq"),
        P("seq", None),
        P(),
    )
    out_specs = (P("win", "seq", None, None), P("win", "seq", None, None))
    return jax.shard_map(body, mesh=mesh, in_specs=in_specs, out_specs=out_specs, check_vma=False)
```

```python
import functools

import jax
import jax.numpy as jnp
from jax import lax
from jax.experimental import pallas as pl
from jax.experimental.pallas import tpu as pltpu
from jax.sharding import PartitionSpec as P

HEAD_DIM = 128
INTERSECTION = 2
STEPS = 50
PERIOD = 40

epsilon = 1e-06
shift_factor = 5.0
bf16 = jnp.bfloat16
f32 = jnp.float32
AXES = ("win", "seq")
NT = (((1,), (1,)), ((), ()))
MIB = 2**20


def place_of(index):
    win, seq = divmod(index, 4)
    y, rest = divmod(win, 8)
    x_hi, z = divmod(rest, 4)
    x_lo, core = divmod(seq, 2)
    return x_hi * 2 + x_lo, y, z, core


def index_of(x, y, z, core):
    x_hi, x_lo = divmod(x % 4, 2)
    return ((y * 2 + x_hi) * 4 + z) * 4 + x_lo * 2 + core


def moves(count, target):
    return [(i, index_of(*target(*place_of(i)))) for i in range(count)]


def to_sibling(x, y, z, core):
    return x, y, z, 1 - core


def to_chip(x, y, z, core):
    return x ^ 1, y, z, core


def to_cross(x, y, z, core):
    return x ^ 1, y, z, 1 - core


def to_far(x, y, z, core):
    return (x - 1 if x % 2 == 0 else x + 1), y, z, core


def to_partner(x, y, z, core):
    return to_chip(x, y, z, core) if core == 0 else to_far(x, y, z, core)


barrier = lax.optimization_barrier


def row_groups(rows):
    return [(start, min(2 * PERIOD, rows - start)) for start in range(0, rows, 2 * PERIOD)]


def tiled(pattern, rows):
    pieces = [pattern] * (rows // PERIOD)
    if rows % PERIOD:
        pieces.append(pattern[: rows % PERIOD])
    return jnp.concatenate(pieces, axis=0) if len(pieces) > 1 else pieces[0]


def normalized(values):
    centered = values - jnp.mean(values, axis=-1, keepdims=True)
    variance = jnp.mean(centered * centered, axis=-1, keepdims=True)
    return centered * lax.rsqrt(variance + epsilon)


def gelu(x):
    inside = x * (0.7978845608028654 + 0.035677408136300125 * (x * x))
    half = 0.5 * x
    return half + half * jnp.tanh(inside)


def in_vmem(count):
    return [pl.BlockSpec(memory_space=pltpu.VMEM)] * count


def params(size):
    return pltpu.CompilerParams(vmem_limit_bytes=size * MIB)


def anywhere(count):
    return [pl.BlockSpec(memory_space=pl.ANY)] * count


def cost(flops, size):
    return pl.CostEstimate(flops=int(flops), bytes_accessed=int(size), transcendentals=0)


def rows_of_frames(steps_ref, table_ref, j):
    frame = lax.broadcasted_iota(jnp.int32, (8, 1), 0)
    vectors = [table_ref[j, pl.ds(steps_ref[0, f], 1), :] for f in range(5)]
    pieces = []
    for part in range(5):
        at = (frame + 8 * part) % 5
        tile = jnp.broadcast_to(vectors[0], (8, vectors[0].shape[1]))
        for f in range(1, 5):
            tile = jnp.where(at == f, vectors[f], tile)
        pieces.append(tile)
    return jnp.concatenate(pieces, axis=0)


def modulation_kernel(steps_ref, table_ref, first_ref, second_ref, last_ref):
    for j in range(6):
        out_ref, at = ((first_ref, j), (second_ref, j - 2), (last_ref, 0))[(j > 1) + (j > 4)]
        out_ref[at] = rows_of_frames(steps_ref, table_ref, j)


def modulation_rows(steps, table):
    return pl.pallas_call(
        modulation_kernel,
        out_shape=[jax.ShapeDtypeStruct((n, PERIOD, table.shape[2]), f32) for n in (2, 3, 1)],
        in_specs=[pl.BlockSpec(memory_space=pltpu.SMEM)] + in_vmem(1),
        out_specs=in_vmem(3),
        compiler_params=params(8),
        name="modulation",
    )(steps, table)


def pack_kernel(frames, lat_ref, out_ref):
    real = lat_ref.shape[0]
    half = out_ref.shape[0]
    lat = lat_ref[:, 0, :]
    lat = jnp.concatenate([lat, lat[real - frames : 2 * half - frames]], axis=0)
    out_ref[...] = jnp.concatenate([lat[:half], lat[half:]], axis=1).astype(bf16)


def pack(lat, rows, frames):
    return pl.pallas_call(
        functools.partial(pack_kernel, frames),
        out_shape=jax.ShapeDtypeStruct((rows // 2, 2 * lat.shape[2]), bf16),
        in_specs=in_vmem(1),
        out_specs=in_vmem(1)[0],
        compiler_params=params(8),
        name="pack",
    )(lat)


def project_block(lat_ref, mod_ref, w_patch_ref, w_qkv_ref, normed_ref, store):
    half, lanes = lat_ref.shape
    channels = lanes // 2
    for side in range(2):
        lat = lat_ref[:, side * channels : (side + 1) * channels]
        embed = jnp.dot(lat, w_patch_ref[...], preferred_element_type=f32)
        normed_ref[side * half : (side + 1) * half, :] = embed
    normed = []
    for start, count in row_groups(2 * half):
        value = normalized(normed_ref[start : start + count, :])
        value = value * (1.0 + tiled(mod_ref[1], count)) + tiled(mod_ref[0], count)
        normed.append(value.astype(bf16))
    normed = jnp.concatenate(normed, axis=0)
    columns = w_qkv_ref.shape[1]
    for c in range(0, columns, 256):
        end = min(c + 256, columns)
        part = jnp.dot(normed, w_qkv_ref[:, c:end], preferred_element_type=f32)
        for d in range(c, end, HEAD_DIM):
            h, j = divmod(d // HEAD_DIM, 3)
            store(h, j, part[:, d - c : d - c + HEAD_DIM])


def store_block(b, real, scale, query_ref, key_ref, value_ref):
    rows = query_ref.shape[0]
    where = slice(b * rows, (b + 1) * rows)

    def store(h, j, piece):
        if j == 0:
            query_ref[:, h * HEAD_DIM : (h + 1) * HEAD_DIM] = (piece * scale).astype(bf16)
        elif j == 1:
            key_ref[h, where, :] = piece.astype(bf16)
        else:
            at = lax.broadcasted_iota(jnp.int32, piece.shape, 0) < real
            value_ref[h, where, :HEAD_DIM] = jnp.where(at, piece, 0.0).astype(bf16)
            value_ref[h, where, HEAD_DIM:] = jnp.where(at, 1.0, 0.0).astype(bf16)

    return store


def project_kernel(blocks, placed, real, scale, after, *refs):
    lat_refs = refs[:blocks]
    mod_ref, w_patch_ref, w_qkv_ref = refs[blocks : blocks + 3]
    refs = refs[blocks + 3 :]
    if placed:
        key_in, value_in = refs[:2]
        refs = refs[2:]
    refs = refs[after:]
    query_refs = refs[:blocks]
    key_ref, value_ref, embed_ref = refs[blocks:]
    rows = query_refs[0].shape[0]
    if placed:
        key_ref[:, : placed * rows, :] = key_in[...]
        value_ref[:, : placed * rows, :] = value_in[...]
    for b in range(blocks):
        store = store_block(placed + b, real, scale, query_refs[b], key_ref, value_ref)
        project_block(lat_refs[b], mod_ref, w_patch_ref, w_qkv_ref, embed_ref.at[b], store)


def project(lats, mods, w_patch, w_qkv, real, scale, before=(), after=()):
    blocks = len(lats)
    rows = 2 * lats[0].shape[0]
    width, columns = w_qkv.shape
    heads = columns // (3 * HEAD_DIM)
    placed = before[0].shape[1] // rows if before else 0
    tokens = (placed + blocks) * rows
    return pl.pallas_call(
        functools.partial(project_kernel, blocks, placed, real, scale, len(after)),
        out_shape=[jax.ShapeDtypeStruct((rows, heads * HEAD_DIM), bf16)] * blocks
        + [
            jax.ShapeDtypeStruct((heads, tokens, HEAD_DIM), bf16),
            jax.ShapeDtypeStruct((heads, tokens, 2 * HEAD_DIM), bf16),
        ],
        in_specs=in_vmem(blocks + 3 + len(before)) + anywhere(len(after)),
        out_specs=in_vmem(blocks + 2),
        scratch_shapes=[pltpu.VMEM((blocks, rows, width), f32)],
        compiler_params=params(8),
        cost_estimate=cost(rows, rows),
        name="project",
    )(*lats, mods, w_patch, w_qkv, *before, *after)


def attend_kernel(blocks, after, *refs):
    query_refs = refs[:blocks]
    key_ref, value_ref = refs[blocks : blocks + 2]
    out_refs = refs[blocks + 2 + after :]
    def scored(query_ref, h):
        query = query_ref[:, h * HEAD_DIM : (h + 1) * HEAD_DIM]
        return lax.dot_general(query, key_ref[h], NT, preferred_element_type=f32)

    heads = key_ref.shape[0]
    for query_ref, out_ref in zip(query_refs, out_refs):
        coming = scored(query_ref, 0)
        for h in range(heads):
            scores = coming
            if h + 1 < heads:
                coming = scored(query_ref, h + 1)
            top = jnp.max(scores, axis=1, keepdims=True)
            weights = jnp.exp2(scores - top).astype(bf16)
            both = jnp.dot(weights, value_ref[h], preferred_element_type=f32)
            columns = slice(h * HEAD_DIM, (h + 1) * HEAD_DIM)
            out_ref[:, columns] = (both[:, :HEAD_DIM] / both[:, HEAD_DIM:]).astype(bf16)


def attend(queries, keys, values, after=()):
    blocks = len(queries)
    rows, width = queries[0].shape
    return pl.pallas_call(
        functools.partial(attend_kernel, blocks, len(after)),
        out_shape=[jax.ShapeDtypeStruct((rows, width), bf16)] * blocks,
        in_specs=in_vmem(blocks + 2) + anywhere(len(after)),
        out_specs=in_vmem(blocks),
        compiler_params=params(8),
        cost_estimate=cost(16 * blocks * rows * width * 4 * rows, 2**20),
        name="attend",
    )(*queries, keys, values, *after)


def output_kernel(a0, a1, a2, a3, w0, w1, w2, w3, lat_ref, mod_ref, w_patch_ref, hid_ref, norm_ref):
    attended = jnp.concatenate([a[...] for a in (a0, a1, a2, a3)], axis=1)
    width = hid_ref.shape[1]
    for c in range(0, width, 256):
        where = slice(c, c + 256)
        weight = jnp.concatenate([w[:, where] for w in (w0, w1, w2, w3)], axis=0)
        total = jnp.dot(attended, weight, preferred_element_type=f32)
        channels = lat_ref.shape[1] // 2
        embed = [
            jnp.dot(lat, w_patch_ref[:, where], preferred_element_type=f32)
            for lat in (lat_ref[:, :channels], lat_ref[:, channels:])
        ]
        embed = jnp.concatenate(embed, axis=0)
        gate = tiled(mod_ref[0, :, where], hid_ref.shape[0])
        hid_ref[:, where] = embed + gate * total
    for start, count in row_groups(hid_ref.shape[0]):
        rows = slice(start, start + count)
        value = normalized(hid_ref[rows, :]) * (1.0 + tiled(mod_ref[2], count))
        norm_ref[rows, :] = (value + tiled(mod_ref[1], count)).astype(bf16)


def output(attended, weights, lat, mods, w_patch):
    shape = (2 * lat.shape[0], w_patch.shape[1])
    return pl.pallas_call(
        output_kernel,
        out_shape=[jax.ShapeDtypeStruct(shape, f32), jax.ShapeDtypeStruct(shape, bf16)],
        in_specs=in_vmem(11),
        out_specs=in_vmem(2),
        compiler_params=params(8),
        cost_estimate=cost(2 * shape[0] * shape[1] ** 2, 2 * shape[1] ** 2),
        name="output",
    )(*attended, *weights, lat, mods, w_patch)


UNITS = 512
COLUMNS = 256


def ffn_kernel(residual, *refs):
    if residual:
        x_ref, hid_ref, mod_ref = refs[:3]
        refs = refs[3:]
    else:
        x_ref = refs[0]
        refs = refs[1:]
    up = refs[0:2]
    down = refs[2:4]
    out_ref, inner_ref = refs[4:]
    units = up[0].shape[0]
    width = x_ref.shape[1]
    for half in range(2):
        for start in range(0, units, UNITS):
            end = min(start + UNITS, units)
            weight = up[half][start:end, :]
            inner = lax.dot_general(x_ref[...], weight, NT, preferred_element_type=f32)
            inner_ref[half, :, start:end] = gelu(inner).astype(bf16)
    for start in range(0, width, COLUMNS):
        where = slice(start, start + COLUMNS)
        value = jnp.dot(inner_ref[0], down[0][:, where], preferred_element_type=f32)
        value += jnp.dot(inner_ref[1], down[1][:, where], preferred_element_type=f32)
        if residual:
            value = hid_ref[:, where] + tiled(mod_ref[0, :, where], x_ref.shape[0]) * value
        out_ref[:, where] = value.astype(out_ref.dtype)


def feed_forward(x, ups, downs, extra=()):
    rows, width = x.shape
    units = ups[0].shape[0]
    return pl.pallas_call(
        functools.partial(ffn_kernel, bool(extra)),
        out_shape=jax.ShapeDtypeStruct(x.shape, bf16 if extra else f32),
        in_specs=in_vmem(5 + len(extra)),
        out_specs=in_vmem(1)[0],
        scratch_shapes=[pltpu.VMEM((2, rows, units), bf16)],
        compiler_params=params(8),
        cost_estimate=cost(8 * rows * width * units, 8 * units * width),
        name="feed_forward",
    )(x, *extra, *ups, *downs)


def head_kernel(steps_ref, table_ref, ffn_ref, hid_ref, w_ref, out_ref, out16_ref):
    gate = rows_of_frames(steps_ref, table_ref, 0)
    rows = ffn_ref.shape[0]
    hidden = hid_ref[...].astype(f32) + tiled(gate, rows) * ffn_ref[...]
    value = normalized(hidden).astype(bf16)
    raw = lax.dot_general(value, w_ref[...], NT, preferred_element_type=f32)
    out_ref[...] = raw
    out16_ref[...] = raw.astype(bf16)


def head(steps, table, ffn, hidden, w_head_t):
    shape = (ffn.shape[0], w_head_t.shape[0])
    return pl.pallas_call(
        head_kernel,
        grid=(1,),
        out_shape=[jax.ShapeDtypeStruct(shape, f32), jax.ShapeDtypeStruct(shape, bf16)],
        in_specs=[
            pl.BlockSpec(memory_space=pltpu.SMEM),
            pl.BlockSpec((1,) + table.shape[1:], lambda i: (5, 0, 0)),
        ]
        + in_vmem(3),
        out_specs=in_vmem(2),
        compiler_params=params(8),
        name="head",
    )(steps, table, ffn, hidden, w_head_t)


def noise_level(step_index):
    fraction = 1.0 - step_index.astype(f32) / STEPS
    return shift_factor * fraction / (1.0 + (shift_factor - 1.0) * fraction)


def join_kernel(windows, frames, steps_ref, lat_ref, raw_ref, before_ref, after_ref, vel_ref, next_ref):
    real, _, channels = lat_ref.shape
    shift = frames - INTERSECTION
    window = lax.axis_index("win")
    frame = lax.broadcasted_iota(jnp.int32, (real, 1), 0) % frames
    steps = jnp.zeros((real, 1), jnp.int32)
    for f in range(frames):
        steps = jnp.where(frame == f, steps_ref[0, f], steps)
    place = frame.astype(f32)
    left = 1.0 - (place + 1.0) / (INTERSECTION + 1.0)
    left = jnp.where((frame < INTERSECTION) & (window > 0), left, 0.0)
    right = 1.0 - (frames - place) / (INTERSECTION + 1.0)
    right = jnp.where((frame >= shift) & (window < windows - 1), right, 0.0)
    none = jnp.zeros((shift, channels), f32)
    before = before_ref[...].astype(f32)
    after = after_ref[...].astype(f32)
    from_left = jnp.concatenate([before[shift:real], none], axis=0)
    from_right = jnp.concatenate([none, after[: real - shift]], axis=0)
    own = 1.0 - left - right
    velocity = own * raw_ref[:real, :] + left * from_left + right * from_right
    vel_ref[:, 0, :] = velocity
    step_size = noise_level(steps + 1) - noise_level(steps)
    next_ref[:, 0, :] = lat_ref[:, 0, :] + step_size * velocity


def join(windows, frames, steps, lat, raw, before, after):
    return pl.pallas_call(
        functools.partial(join_kernel, windows, frames),
        out_shape=[jax.ShapeDtypeStruct(lat.shape, f32)] * 2,
        in_specs=[pl.BlockSpec(memory_space=pltpu.SMEM)] + in_vmem(4),
        out_specs=in_vmem(2),
        compiler_params=params(8),
        name="join",
    )(steps, lat, raw, before, after)


def body(latent, frame_steps, mod_table, w_patch, w_qkv, w_out, w_ff1, w_ff2, w_head):
    _, patches, frames, channels = latent.shape
    windows = lax.axis_size("win")
    devices = windows * lax.axis_size("seq")
    real = patches * frames
    rows = -(-real // 16) * 16
    heads = w_out.shape[0] // HEAD_DIM

    def send(value, target):
        return lax.ppermute(value, AXES, moves(devices, target))

    flat = jnp.transpose(latent, (1, 2, 0, 3)).reshape(real, 1, channels)
    lat = pack(flat, rows, frames)
    lat_sib = send(lat, to_sibling)
    lat_chip = send(lat, to_chip)
    lat_cross = send(lat, to_cross)

    table = jnp.transpose(mod_table, (1, 0, 2))
    first_mods, second_mods, last_mods = modulation_rows(frame_steps, table)

    up = w_ff1.T
    lat_sib, lat_chip, lat_cross, first_mods, up_near, down_near, out_near = barrier(
        (lat_sib, lat_chip, lat_cross, first_mods, up, w_ff2, w_out)
    )
    out_chip = send(out_near, to_partner)
    up_sib = send(up_near, to_sibling)
    down_sib = send(down_near, to_sibling)

    scale = HEAD_DIM**-0.5 * 1.4426950408889634
    query_own, query_sib, keys, values = project(
        [lat, lat_sib], first_mods, w_patch, w_qkv, real, scale
    )
    query_chip, query_cross, keys, values = project(
        [lat_chip, lat_cross], first_mods, w_patch, w_qkv, real, scale, (keys, values)
    )
    (att_cross,) = attend([query_cross], keys, values, (up_sib,))
    got_cross = send(att_cross, to_cross)
    (att_chip,) = attend([query_chip], keys, values)
    got_chip = send(att_chip, to_chip)
    (att_sib,) = attend([query_sib], keys, values, (att_cross, att_chip))
    (att_own,) = attend([query_own], keys, values, (att_sib, down_sib))
    out_chip, _, out_near = barrier((out_chip, att_chip, w_out))
    _, steps_near = barrier((att_own, frame_steps))
    got_sib = send(att_sib, to_sibling)
    out_cross = send(out_chip, to_sibling)
    out_sib = send(out_near, to_sibling)
    steps_partner = send(steps_near, to_partner)

    hidden1, normed2 = output(
        (att_own, got_sib, got_chip, got_cross),
        (w_out, out_sib, out_chip, out_cross),
        lat,
        second_mods,
        w_patch,
    )
    normed_partner = send(normed2, to_partner)
    ups, downs = (up, up_sib), (w_ff2, down_sib)
    hidden_near = feed_forward(normed2, ups, downs, (hidden1, last_mods))
    hidden_partner = send(hidden_near, to_partner)
    ffn_partner = feed_forward(normed_partner, ups, downs)
    raw_partner, raw16 = head(steps_partner, table, ffn_partner, hidden_partner, w_head.T)

    owner = [to for _, to in moves(devices, to_partner)]
    up_next = [(i, owner[i] + 4) for i in range(devices) if owner[i] + 4 < devices]
    down_next = [(i, owner[i] - 4) for i in range(devices) if owner[i] - 4 >= 0]
    before = lax.ppermute(raw16, AXES, up_next)
    after = lax.ppermute(raw16, AXES, down_next)
    raw = send(raw_partner, to_partner)
    velocity, latent_next = join(windows, frames, frame_steps, flat, raw, before, after)

    def as_argument(value):
        return jnp.transpose(value.reshape(patches, frames, 1, channels), (2, 0, 1, 3))

    return as_argument(velocity), as_argument(latent_next)


def solution(mesh):
    in_specs = (
        P("win", "seq", None, None),
        P("win", None),
        P(),
        P(),
        P(None, "seq"),
        P("seq", None),
        P(None, "seq"),
        P("seq", None),
        P(),
    )
    out_specs = (P("win", "seq", None, None), P("win", "seq", None, None))
    return jax.shard_map(body, mesh=mesh, in_specs=in_specs, out_specs=out_specs, check_vma=False)
```
